32 devices in a mesh: region: 16 (over z, y, core), sub: 2 (over x).
Axes of the slice: x: 2, y: 2, z: 4, core: 2. Of those that a mesh axis runs over, the one named last changes fastest.
Arguments:
- sources: bfloat16 [32, 2048, 1280], P(('region', 'sub')), may hold values from -6 to 6
- coupling: bfloat16 [32, 2048, 2048], P(('region', 'sub')), may hold values from -0.0625 to 0.0625
- self_term: float32 [32, 2048], P(('region', 'sub')), may hold values from 0.25 to 1
- history: float32 [32, 4, 8, 640], P(('region', 'sub')), may hold values from -6 to 6
- line_nodes: int32 [32, 4, 8], P(('region', 'sub')), may hold values from -1 to 2047, as said below
- line_admit: float32 [32, 4, 8], P(('region', 'sub')), may hold values from 0 to 1, as said below
- term_region: int32 [8192, 1], P(('region', 'sub')), may hold values from 0 to 15; in each aligned block of 256 rows (0 to 255, 256 to 511, ...) at most 32 rows name the same one
- old_samples: bfloat16 [8192, 1280], P(('region', 'sub')), may hold values from -6 to 6
- prior_phasor: float32 [8192, 2, 128], P(('region', 'sub')), may hold values from -6 to 6
Outputs:
- next_history: float32 [32, 4, 8, 640], P(('region', 'sub'))
- node_voltages: bfloat16 [32, 2048, 1280], P(('region', 'sub'))
- phasors: float32 [16384, 2, 2, 128], P(('region', 'sub'))
The draws below stay inside these ranges and needn't reach their ends.
Inputs may be any that keep to these rules, and one draw needn't show every extreme that they name: line_nodes[a, d, k] is -1 for an empty slot and for every slot of a direction with no subsystem; each subsystem has lines to each of its up to 4 neighbours in the directions of the steps, 1 to 8 lines a pair, in the first slots; [a, d, k] and the slot k of the opposite direction at the neighbour are both -1 or are the two ends of one line; some pair uses all 8 slots. line_admit is equal at the two ends of a line; it is 0 exactly where line_nodes is -1, else 0.25 or more. `term_region`: among the 256 terminals of one subsystem at most 32 name the same region, and in every draw some region is named by exactly 32 of one subsystem's terminals.
All inputs are finite; a program needn't handle non-finite values.
Results may differ from the reference program's by a relative error of at most 0.003.
Values sent between devices are 32-bit elements; how exact they have to be, the bound alone decides.
No kernel may reach another device: no remote copies, remote signals or barrier semaphores. Data moves between devices by JAX's collectives and lax.ppermute only.
A program may use at most 128 MiB of HBM per device.

```python
import math
import jax
import jax.numpy as jnp
import numpy as np
from jax import lax

NODES = 2048
NEIGH = 4
LPP = 8
DELAY = 40
SPANS = 2
SCEN = 16
TERM_DEV = 256
BINS = 8
DFT_LEN = 2048
SUBSYSTEMS = 32
STEPS = 80
CAP = 32
TERMINALS = 8192
N_REGION = 16
N_SUB = 2


def spread_edges(sub_edges, region_edges):
    sub_pad = jnp.pad(sub_edges, ((0, 0), (1, 1)) + ((0, 0),) * (sub_edges.ndim - 2))
    region_pad = jnp.pad(region_edges, ((1, 1), (0, 0)) + ((0, 0),) * (region_edges.ndim - 2))
    toward_lower_sub = sub_pad[:, :N_SUB]
    toward_upper_sub = sub_pad[:, 1:N_SUB + 1]
    toward_lower_region = region_pad[:N_REGION]
    toward_upper_region = region_pad[1:N_REGION + 1]
    stacked = jnp.stack([toward_lower_sub, toward_upper_sub, toward_lower_region, toward_upper_region], axis=2)
    return stacked.reshape((N_REGION * N_SUB, NEIGH) + stacked.shape[3:])


def line_tables(key):
    key_subc = jax.random.fold_in(key, 21)
    key_regc = jax.random.fold_in(key, 22)
    key_pick = jax.random.fold_in(key, 23)
    key_nodes = jax.random.fold_in(key, 24)
    key_suba = jax.random.fold_in(key, 25)
    key_rega = jax.random.fold_in(key, 26)
    sub_counts = jax.random.randint(key_subc, (N_REGION, N_SUB - 1), 1, LPP + 1)
    region_counts = jax.random.randint(key_regc, (N_REGION - 1, N_SUB), 1, LPP + 1)
    chosen = jax.random.randint(key_pick, (), 0, N_REGION * (N_SUB - 1))
    flat_index = jnp.arange(N_REGION * (N_SUB - 1)).reshape(N_REGION, N_SUB - 1)
    sub_counts = jnp.where(flat_index == chosen, LPP, sub_counts)
    counts = spread_edges(sub_counts, region_counts)
    slots = jnp.arange(LPP)
    live_slot = slots[None, None, :] < counts[:, :, None]
    end_nodes = jax.random.randint(key_nodes, (N_REGION * N_SUB, NEIGH, LPP), 0, NODES)
    end_nodes = jnp.where(live_slot, end_nodes, -1).astype(jnp.int32)
    sub_admit = jax.random.uniform(key_suba, (N_REGION, N_SUB - 1, LPP), jnp.float32)
    region_admit = jax.random.uniform(key_rega, (N_REGION - 1, N_SUB, LPP), jnp.float32)
    mirrored = spread_edges(sub_admit, region_admit)
    admit = jnp.where(live_slot, 0.25 * jnp.exp(jnp.log(4.0) * mirrored), 0.0).astype(jnp.float32)
    return (end_nodes, admit)


def draw_line_nodes(key, part):
    return line_tables(key)[0]


def draw_line_admit(key, part):
    return line_tables(key)[1]


def block_levels(key, shape, cuts, least, top_value):
    def one(axis_at, blocks):
        draws = jax.random.uniform(jax.random.fold_in(jax.random.fold_in(key, 6), axis_at), (blocks,), jnp.float32, least / len(cuts), top_value / len(cuts))
        return jnp.repeat(jnp.exp(draws), shape[axis_at] // blocks).reshape((-1,) + (1,) * (len(shape) - axis_at - 1))

    factor_of = one(*cuts[0])
    for cut in cuts[1:]:
        factor_of = factor_of * one(*cut)
    return factor_of


def routed_block(own_key, own, number, rows, number_of, top, reach, lean):
    order = jax.random.permutation(own_key, number_of)
    heavy_load, ordinary = shares(number_of, rows * top, reach, lean, True), shares(number_of, rows * top, reach, lean, False)
    places = jnp.arange(number_of)

    def named(lengths, offset_by):
        used = int((lengths > 0).sum())
        fixed = max(1, used // 4)
        moved = fixed + (places - fixed + offset_by * (used - fixed)) % max(1, number_of - fixed)
        return jnp.zeros((number_of,), jnp.int32).at[order[jnp.where(places < fixed, places, moved)]].set(jnp.asarray(lengths, jnp.int32))

    lengths = jnp.where(number % 4 == 0, named(heavy_load, number // 4), named(ordinary, number - number // 4 - 1))
    mixed = jax.random.permutation(jax.random.fold_in(own, 3), number_of)
    donor, receiver = mixed[0:number_of // 2 * 2:2], mixed[1:number_of // 2 * 2:2]
    slack = jnp.minimum(lengths[donor] - 1, reach - lengths[receiver]) // 2
    slack = jnp.where((donor == order[0]) | (receiver == order[0]) | (lengths[receiver] == 0), 0, jnp.maximum(slack, 0))
    moved = jax.random.randint(jax.random.fold_in(own, 4), (number_of // 2,), 0, 1 << 20) % (slack + 1)
    lengths = lengths.at[donor].add(-moved).at[receiver].add(moved)
    items = jnp.searchsorted(jnp.cumsum(lengths), jnp.arange(rows * top), side="right").astype(jnp.int32)
    listing = items.reshape(top, rows).T
    listing = listing[jax.random.permutation(jax.random.fold_in(own, 1), rows)]
    offset_by = jax.random.randint(jax.random.fold_in(own, 2), (rows, 1), 0, top)
    return jnp.take_along_axis(listing, (jnp.arange(top)[None, :] + offset_by) % top, axis=1)


def shares(amount, total, bound, lean, full):
    weights = [(1 << 20) // math.isqrt(standing ** lean) + 1 for standing in range(1, amount + 1)]
    largest = bound if full else min(bound, max(-(-total // amount), total * weights[0] // sum(weights)))
    least = 1 if total - largest >= amount - 1 else 0
    given, spare = [largest] + [least] * (amount - 1), total - largest - least * (amount - 1)
    while spare > 0:
        free = [i for i in range(1, amount) if given[i] < largest] or [i for i in range(1, amount) if given[i] < bound]
        whole, left = sum([weights[i] for i in free]), spare
        for i in free:
            more = min(bound - given[i], max(1, left * weights[i] // whole), spare)
            given[i] = given[i] + more
            spare = spare - more
    return np.array(given)


def centred(rng, dims, spread, reach, cuts=(), held_as=jnp.bfloat16):
    array = spread * jax.random.normal(rng, dims, jnp.float32)
    if cuts:
        array = array * block_levels(rng, dims, cuts, -0.22, 0.18)
    return jnp.clip(array, -reach, reach).astype(held_as)


def setup_inputs(seed: int = 0) -> dict:
    arg_keys = jax.random.split(jax.random.key(seed), 10)
    sources = centred(arg_keys[0], (SUBSYSTEMS, NODES, STEPS * SCEN), 1.0, 6.0, ((0, 32),))
    coupling = centred(arg_keys[1], (SUBSYSTEMS, NODES, NODES), (4 * NODES) ** -0.5, 0.0625, ((0, 32),))
    self_term = jnp.clip(jnp.exp(math.log(1.0) - 1.3862944 * jax.random.uniform(arg_keys[2], (SUBSYSTEMS, NODES), jnp.float32) ** block_levels(arg_keys[2], (SUBSYSTEMS, NODES), ((0, 32),), -0.2, 0.2)), 0.25, 1.0)
    history = centred(arg_keys[3], (SUBSYSTEMS, NEIGH, LPP, DELAY * SCEN), 1.0, 6.0, ((0, 32),), jnp.float32)
    line_nodes = draw_line_nodes(jax.random.fold_in(arg_keys[9], 71), 0)
    line_admit = draw_line_admit(jax.random.fold_in(arg_keys[9], 71), 0)
    term_region_keys = jax.random.split(jax.random.fold_in(arg_keys[6], 1), TERMINALS // TERM_DEV)
    term_region_turns = jax.random.permutation(jax.random.fold_in(arg_keys[6], 3), TERMINALS // TERM_DEV)
    term_region = jax.vmap(lambda own, number: routed_block(jax.random.fold_in(arg_keys[6], 2), own, number, TERM_DEV, N_REGION, 1, CAP, 2))(term_region_keys, term_region_turns).reshape((TERMINALS, 1))
    old_samples = centred(arg_keys[7], (TERMINALS, STEPS * SCEN), 1.0, 6.0, ((0, 32),))
    prior_phasor = centred(arg_keys[8], (TERMINALS, 2, BINS * SCEN), 1.0, 6.0, ((0, 32),), jnp.float32)
    return dict(sources=sources, coupling=coupling, self_term=self_term, history=history, line_nodes=line_nodes, line_admit=line_admit, term_region=term_region, old_samples=old_samples, prior_phasor=prior_phasor)


def phasor_fit(differences, prior):
    row_count = differences.shape[0]
    blocks = differences.reshape(row_count, SPANS, DELAY, SCEN)
    step_index = jnp.arange(SPANS * DELAY, dtype=jnp.int32).reshape(SPANS, DELAY)
    harmonic = jnp.arange(1, BINS + 1, dtype=jnp.int32)
    product = step_index[:, :, None] * harmonic[None, None, :] % DFT_LEN
    angles = product.astype(differences.dtype) * (2.0 * math.pi / DFT_LEN)
    norm_scale = 1.0 / math.sqrt(DFT_LEN)
    twiddle = jnp.stack([jnp.cos(angles), -jnp.sin(angles)], axis=2) * norm_scale
    partial_value = jnp.einsum('ajts,jtch->ajchs', blocks, twiddle.astype(differences.dtype), precision=lax.Precision.HIGHEST)
    running = jnp.cumsum(partial_value, axis=1).reshape(row_count, SPANS, 2, BINS * SCEN)
    return running + prior[:, None]

def route_lines(outgoing):
    span_cols = outgoing.shape[-1]
    grid = outgoing.reshape(N_REGION, N_SUB, NEIGH, LPP, span_cols)
    no_pad = (0, 0)
    from_lower_sub = jnp.pad(grid[:, :-1, 1], (no_pad, (1, 0), no_pad, no_pad))
    from_upper_sub = jnp.pad(grid[:, 1:, 0], (no_pad, (0, 1), no_pad, no_pad))
    from_lower_region = jnp.pad(grid[:-1, :, 3], ((1, 0), no_pad, no_pad, no_pad))
    from_upper_region = jnp.pad(grid[1:, :, 2], ((0, 1), no_pad, no_pad, no_pad))
    arrived = jnp.stack([from_lower_sub, from_upper_sub, from_lower_region, from_upper_region], axis=2)
    return arrived.reshape(N_REGION * N_SUB, NEIGH, LPP, span_cols)

def reference(sources, coupling, self_term, history, line_nodes, line_admit, term_region, old_samples, prior_phasor):
    peers = N_REGION * N_SUB
    span_cols = DELAY * SCEN
    live_slot = line_nodes >= 0
    incoming = history
    pieces = []
    node_pieces = []
    for span_index in range(SPANS):
        span_src = sources[:, :, span_index * span_cols:(span_index + 1) * span_cols]

        def per_device(items):
            matrix, self_gain, block_src, arrived, end_nodes, live_row, admit_row = items
            end_flat = end_nodes.reshape(-1)
            live_flat = live_row.reshape(-1)
            line_rows = arrived.reshape(NEIGH * LPP, span_cols)
            target = jnp.where(live_flat, end_flat, NODES)
            injection = jnp.zeros((NODES, span_cols), jnp.float32).at[target].add(line_rows, mode='drop').astype(jnp.bfloat16)
            voltages = jnp.dot(matrix, block_src, preferred_element_type=jnp.float32)
            voltages = voltages + jnp.dot(matrix, injection, preferred_element_type=jnp.float32)
            voltages = voltages + self_gain[:, None] * (block_src.astype(jnp.float32) + injection.astype(jnp.float32))
            pick_rows = jnp.where(live_flat, end_flat, 0)
            line_volts = voltages[pick_rows]
            outgoing = jnp.where(live_flat[:, None], 2.0 * admit_row.reshape(-1, 1) * line_volts - line_rows, 0.0)
            return (outgoing.reshape(NEIGH, LPP, span_cols), voltages[:TERM_DEV], voltages.astype(jnp.bfloat16))
        outgoing, terminal_volts, all_volts = lax.map(per_device, (coupling, self_term, span_src, incoming, line_nodes, live_slot, line_admit))
        incoming = route_lines(outgoing)
        pieces.append(terminal_volts)
        node_pieces.append(all_volts)
    node_voltages = jnp.concatenate(node_pieces, axis=2)
    waveforms = jnp.concatenate(pieces, axis=2).reshape(peers * TERM_DEV, STEPS * SCEN)
    differences = waveforms - old_samples.astype(jnp.float32)
    fitted = phasor_fit(differences, prior_phasor)
    regions = term_region[:, 0].reshape(peers, TERM_DEV)
    onehot = (regions[:, :, None] == jnp.arange(N_REGION, dtype=jnp.int32)[None, None, :]).astype(jnp.int32)
    rank_in = jnp.cumsum(onehot, axis=1) - onehot
    slot_index = lax.optimization_barrier(jnp.sum(rank_in * onehot, axis=2))
    device_index = jnp.arange(peers, dtype=jnp.int32)[:, None]
    src_region = device_index // N_SUB
    src_sub = device_index % N_SUB
    dest_row = ((regions * N_SUB + src_sub) * N_REGION + src_region) * CAP + slot_index
    phasors = jnp.zeros((peers * N_REGION * CAP, SPANS, 2, BINS * SCEN), jnp.float32)
    phasors = phasors.at[dest_row.reshape(-1).astype(jnp.int32)].set(fitted)
    return (incoming, node_voltages, phasors)
```

```python
import functools
import math

import jax
import jax.numpy as jnp
import numpy as np
from jax import lax
from jax.experimental import pallas as pl
from jax.experimental.pallas import tpu as pltpu
from jax.sharding import PartitionSpec as P

NODES = 2048
NEIGH = 4
LPP = 8
DELAY = 40
SPANS = 2
SCEN = 16
TERM_DEV = 256
BINS = 8
DFT_LEN = 2048

LINES = NEIGH * LPP
COLS = DELAY * SCEN
LANES = 128
PHASOR = 2 * BINS * SCEN
ROWS = 256
VMEM_LIMIT = 24 * 1024 * 1024

F32 = jnp.float32
BF16 = jnp.bfloat16


def fit_tables():
    step = np.arange(SPANS * DELAY)
    harmonic = np.arange(1, BINS + 1)
    angles = (step[:, None] * harmonic[None, :] % DFT_LEN) * (2.0 * math.pi / DFT_LEN)
    twiddle = np.stack([np.cos(angles), -np.sin(angles)], axis=1) / math.sqrt(DFT_LEN)
    table = np.einsum("uch,st->uscht", twiddle, np.eye(SCEN))
    table = table.reshape(SPANS * COLS, PHASOR).astype(np.float32)
    high = table.astype(jnp.bfloat16)
    low = (table - high.astype(np.float32)).astype(jnp.bfloat16)
    return np.concatenate([high, low], axis=1)


def dot(left, right):
    return jnp.dot(left, right, preferred_element_type=F32)


def split(value):
    high = value.astype(BF16)
    return high, (value - high.astype(F32)).astype(BF16)


def fit(values, table):
    high, low = split(values)
    both = dot(high, table)
    return both[:, :PHASOR] + both[:, PHASOR:] + dot(low, table[:, :PHASOR])


def iota(shape, axis):
    return lax.broadcasted_iota(jnp.int32, shape, axis)


def slot_vectors(nodes_ref):
    lane = iota((1, LANES), 1)
    row_id = iota((LINES, 1), 0)
    along = jnp.full((1, LANES), -1, jnp.int32)
    down = jnp.full((LINES, 1), -1, jnp.int32)
    for slot in range(LINES):
        node = nodes_ref[slot // LPP, slot % LPP]
        hit = (lane == slot) | (lane == slot + LINES) | (lane == slot + 2 * LINES)
        along = jnp.where(hit, node, along)
        down = jnp.where(row_id == slot, node, down)
    return along, down


def slot_column(value_ref):
    row_id = iota((LINES, 1), 0)
    down = jnp.zeros((LINES, 1), F32)
    for slot in range(LINES):
        down = jnp.where(row_id == slot, value_ref[slot // LPP, slot % LPP], down)
    return down


def first_slots(along, down):
    lane = iota((LINES, LANES), 1)
    row_id = iota((LINES, LANES), 0)
    same = (down == along) & (down >= 0)
    before = jnp.where(same & (row_id < lane % LINES), 1, 0)
    first_along = (jnp.sum(before, axis=0, keepdims=True) == 0) & (along >= 0)
    after = jnp.where(same & (lane < row_id), 1, 0)
    first_down = (jnp.sum(after, axis=1, keepdims=True) == 0) & (down >= 0)
    return first_along, first_down


def injected(lines, along, down):
    same = ((down == along) & (down >= 0))[:, :LINES]
    pick = jnp.where(same, 1.0, 0.0).astype(BF16)
    high = lines.astype(BF16)
    mid, low = split(lines - high.astype(F32))
    total = dot(pick, high) + (dot(pick, mid) + dot(pick, low))
    return total.astype(BF16)


def one_hot(along, rows, offset=0):
    lane = iota((1, LANES), 1)
    wanted = jnp.where(lane < LINES, along, -1)
    return jnp.where(iota((rows, LANES), 0) + offset == wanted, 1.0, 0.0).astype(BF16)


def three_times(rows):
    width = rows.shape[1]
    return jnp.concatenate([rows, rows, rows, jnp.zeros((LANES - 3 * LINES, width), rows.dtype)], axis=0)


def column_of(row):
    size = row.shape[1]
    eye = iota((size, size), 0) == iota((size, size), 1)
    return jnp.sum(jnp.where(eye, row, 0.0), axis=1, keepdims=True)


def small_left(gathered, self_col, along, first_along, offset):
    rows = gathered.shape[0]
    lane = iota((1, LANES), 1)
    high, low = split(self_col)
    here = (iota((rows, LANES), 0) + offset == along) & first_along & (lane >= LINES)
    weight = jnp.where(lane < 2 * LINES, high.astype(F32), low.astype(F32))
    return (gathered + jnp.where(here, weight, 0.0)).astype(BF16)


def outgoing_of(volts, lines, admit_ref, down):
    value = 2.0 * slot_column(admit_ref) * volts - lines
    return jnp.where(down >= 0, value, 0.0)


def send_out(outgoing, place_ref, sub_ref, near_ref, far_ref):
    odd_region = place_ref[0] == 1
    odd_sub = place_ref[1] == 1
    lower_sub, upper_sub = outgoing[:LPP], outgoing[LPP : 2 * LPP]
    lower, upper = outgoing[2 * LPP : 3 * LPP], outgoing[3 * LPP :]
    sub_ref[...] = jnp.where(odd_sub, lower_sub, upper_sub)
    near_ref[...] = jnp.where(odd_region, lower, upper)
    far_ref[...] = jnp.where(odd_region, upper, lower)


def lines_kernel(
    place_ref, nodes_ref, admit_ref, self_ref, history_ref, coupling_ref, sources_ref,
    sub_ref, near_ref, far_ref, rows_ref, inj_ref,
    src_buf, blocks, src_sem, block_sem,
):
    chunks = 4
    depth = NODES // chunks

    def src_copy(part):
        rows = pl.ds(part * depth, depth)
        return pltpu.make_async_copy(
            sources_ref.at[0, rows, pl.ds(0, COLS)], src_buf.at[rows], src_sem.at[part]
        )

    def block_copy(slot):
        node = jnp.maximum(nodes_ref[slot // LPP, slot % LPP], 0)
        start = pl.multiple_of((node // 16) * 16, 16)
        return pltpu.make_async_copy(
            coupling_ref.at[0, pl.ds(start, 16)], blocks.at[pl.ds(slot * 16, 16)], block_sem.at[slot]
        )

    for slot in range(LINES):
        block_copy(slot).start()
    for part in range(chunks):
        src_copy(part).start()

    along, down = slot_vectors(nodes_ref)
    first_along, first_down = first_slots(along, down)
    lines = history_ref[0].reshape(LINES, COLS)
    total = injected(lines, along, down)
    injection = jnp.where(first_down, total, jnp.zeros_like(total))
    inj_ref[...] = injection
    at_node = jnp.maximum(down, 0)
    choose = jnp.where(
        iota((LINES, LINES * 16), 1) == iota((LINES, LINES * 16), 0) * 16 + at_node % 16, 1.0, 0.0
    ).astype(BF16)
    own_row = iota((LINES, NODES), 1) == at_node
    own = jnp.where(own_row, 1.0, 0.0).astype(BF16)
    self_col = jnp.sum(jnp.where(own_row, self_ref[...], 0.0), axis=1, keepdims=True)
    hot = one_hot(along, NODES)

    for slot in range(LINES):
        block_copy(slot).wait()
    rows = dot(choose, blocks[...]).astype(BF16)
    rows_ref[...] = rows
    gathered = dot(rows, hot)
    volts = dot(gathered.astype(BF16)[:, :LINES], injection)
    left = jnp.concatenate([rows, own], axis=0)
    picked = jnp.zeros((2 * LINES, COLS), F32)
    for part in range(chunks):
        src_copy(part).wait()
        span = slice(part * depth, (part + 1) * depth)
        picked = picked + dot(left[:, span], src_buf[span, :])
    volts = volts + picked[:LINES] + self_col * (picked[LINES:] + total.astype(F32))
    send_out(outgoing_of(volts, lines, admit_ref, down), place_ref, sub_ref, near_ref, far_ref)


def terminals_kernel(
    capacity, slots,
    nodes_ref, self_ref, rows_ref, inj_ref, region_ref, prior_ref, old_ref, table_ref,
    coupling_ref, sources_ref,
    packed_ref, left_ref, gathered_ref, base_ref,
    src_buf, left_buf, src_sem, left_sem,
):
    chunks = 8
    depth = NODES // chunks

    def src_copy(part):
        rows = pl.ds(part * depth, depth)
        return pltpu.make_async_copy(
            sources_ref.at[0, rows], src_buf.at[rows], src_sem.at[part]
        )

    left_copy = pltpu.make_async_copy(
        coupling_ref.at[0, pl.ds(0, TERM_DEV)], left_buf.at[pl.ds(0, TERM_DEV)], left_sem
    )
    left_copy.start()
    for part in range(chunks):
        src_copy(part).start()

    along, down = slot_vectors(nodes_ref)
    first_along, _ = first_slots(along, down)
    at_node = jnp.maximum(down, 0)
    own_row = iota((LINES, NODES), 1) == at_node
    left_buf[TERM_DEV : TERM_DEV + LINES, :] = rows_ref[...]
    left_buf[TERM_DEV + LINES :, :] = jnp.where(own_row, 1.0, 0.0).astype(BF16)
    line_self = jnp.sum(jnp.where(own_row, self_ref[...], 0.0), axis=1, keepdims=True)
    term_self = column_of(self_ref[:, :TERM_DEV])
    hot = one_hot(along, NODES)

    region_row = region_ref[...]
    region_col = column_of(region_row.astype(F32)).astype(jnp.int32)
    earlier = iota((TERM_DEV, TERM_DEV), 0) < iota((TERM_DEV, TERM_DEV), 1)
    rank = jnp.sum(
        jnp.where((region_col == region_row) & earlier, 1, 0), axis=0, keepdims=True
    )
    dest = region_row * capacity + rank
    pack = jnp.where(iota((slots, TERM_DEV), 0) == dest, 1.0, 0.0).astype(BF16)

    left_copy.wait()
    gathered = dot(left_buf[: TERM_DEV + LINES, :], hot)
    gathered_ref[...] = gathered[TERM_DEV:].astype(BF16)
    small = small_left(gathered[:TERM_DEV], term_self, along, first_along, 0)
    left_ref[...] = dot(pack, small).astype(BF16)
    total = jnp.zeros((TERM_DEV + 2 * LINES, SPANS * COLS), F32)
    for part in range(chunks):
        src_copy(part).wait()
        span = slice(part * depth, (part + 1) * depth)
        total = total + dot(left_buf[:, span], src_buf[span, :])
    lines_at = total[TERM_DEV : TERM_DEV + LINES, COLS:]
    base_ref[...] = lines_at + line_self * total[TERM_DEV + LINES :, COLS:]
    volts = total[:TERM_DEV] + term_self * src_buf[:TERM_DEV, :].astype(F32)
    differences = volts - old_ref[...].astype(F32)
    from_lines = dot(small, three_times(inj_ref[...]))
    running = prior_ref[...].reshape(TERM_DEV, 2, LANES)
    running = jnp.concatenate([running[:, 0], running[:, 1]], axis=1)
    for span_index in range(SPANS):
        cols = slice(span_index * COLS, (span_index + 1) * COLS)
        values = differences[:, cols]
        if span_index == 0:
            values = values + from_lines
        running = running + fit(values, table_ref[cols, :])
        high, low = split(running)
        filled = dot(pack, high) + dot(pack, low)
        for part in range(2):
            packed_ref[pl.ds(2 * span_index + part, slots, stride=4), :] = filled[
                :, part * LANES : (part + 1) * LANES
            ]


def second_kernel(
    slots,
    place_ref, nodes_ref, admit_ref, self_ref, from_sub_ref, from_near_ref, from_far_ref,
    base_ref, gathered_ref, left_ref, table_ref, packed_in_ref,
    packed_ref, sub_ref, near_ref, far_ref, inj_ref,
):
    along, down = slot_vectors(nodes_ref)
    _, first_down = first_slots(along, down)
    odd_region = place_ref[0] == 1
    odd_sub = place_ref[1] == 1
    from_sub, near, far = from_sub_ref[...], from_near_ref[...], from_far_ref[...]
    none = jnp.zeros_like(from_sub)
    lines = jnp.concatenate(
        [
            jnp.where(odd_sub, from_sub, none),
            jnp.where(odd_sub, none, from_sub),
            jnp.where(odd_region, near, far),
            jnp.where(odd_region, far, near),
        ],
        axis=0,
    )
    total = injected(lines, along, down)
    injection = jnp.where(first_down, total, jnp.zeros_like(total))
    inj_ref[...] = injection
    both = dot(injection, table_ref[...])
    spectrum = both[:, :PHASOR] + both[:, PHASOR:]
    high, low = split(spectrum)
    left = left_ref[...]
    change = dot(left, three_times(high)) + dot(left, three_times(low))
    for row in range(2):
        rows = pl.ds(row, slots, stride=4)
        packed_ref[rows, :] = packed_in_ref[rows, :]
    for part in range(2):
        rows = pl.ds(2 + part, slots, stride=4)
        packed_ref[rows, :] = packed_in_ref[rows, :] + change[:, part * LANES : (part + 1) * LANES]
    own_row = iota((LINES, NODES), 1) == jnp.maximum(down, 0)
    self_col = jnp.sum(jnp.where(own_row, self_ref[...], 0.0), axis=1, keepdims=True)
    volts = base_ref[...] + dot(gathered_ref[:, :LINES], injection) + self_col * total.astype(F32)
    send_out(outgoing_of(volts, lines, admit_ref, down), place_ref, sub_ref, near_ref, far_ref)


def nodes_kernel(
    nodes_ref, self_ref, inj0_ref, inj1_ref, coupling_ref, sources_ref, volts_ref,
    hot_buf, small_buf,
):
    step = pl.program_id(0)
    along, down = slot_vectors(nodes_ref)
    first_along, _ = first_slots(along, down)

    @pl.when(step == 0)
    def _():
        hot_buf[...] = one_hot(along, NODES)
        rows = jnp.concatenate([inj0_ref[...], inj1_ref[...]], axis=1)
        small_buf[...] = three_times(rows)

    start = pl.multiple_of(step * ROWS, ROWS)
    matrix = coupling_ref[0]
    gathered = dot(matrix, hot_buf[...])
    self_col = column_of(self_ref[:, pl.ds(start, ROWS)])
    small = small_left(gathered, self_col, along, first_along, start)
    total = dot(matrix, sources_ref[0]) + dot(small, small_buf[...])
    total = total + self_col * sources_ref[0, pl.ds(start, ROWS), :].astype(F32)
    volts_ref[0] = total.astype(BF16)


def vmem(*shape_dtype):
    return pl.BlockSpec(memory_space=pltpu.VMEM)


VM = pl.BlockSpec(memory_space=pltpu.VMEM)
SM = pl.BlockSpec(memory_space=pltpu.SMEM)
ANY = pl.BlockSpec(memory_space=pl.ANY)


def struct(shape, dtype):
    return jax.ShapeDtypeStruct(shape, dtype)


def params():
    return pltpu.CompilerParams(vmem_limit_bytes=VMEM_LIMIT)


def exchange(sub, near, far):
    subs = lax.axis_size("sub")
    regions = lax.axis_size("region")

    def swap(block, axis, size, first):
        pairs = []
        for low in range(first, size - 1, 2):
            pairs += [(low, low + 1), (low + 1, low)]
        return lax.ppermute(block, axis, pairs)

    return (
        swap(near, "region", regions, 0),
        swap(sub, "sub", subs, 0),
        swap(far, "region", regions, 1),
    )


def body(
    sources,
    coupling,
    self_term,
    history,
    line_nodes,
    line_admit,
    term_region,
    old_samples,
    prior_phasor,
):
    region_count = lax.axis_size("region")
    capacity = max(2, 2 * TERM_DEV // region_count)
    slots = region_count * capacity
    odd_region = lax.axis_index("region") % 2
    odd_sub = lax.axis_index("sub") % 2
    place = jnp.stack([odd_region, odd_sub]).astype(jnp.int32)
    nodes = line_nodes[0]
    admit = line_admit[0]
    tables = fit_tables()
    block = struct((LPP, COLS), F32)

    sub, near, far, rows, inj0 = pl.pallas_call(
        lines_kernel,
        out_shape=[block, block, block, struct((LINES, NODES), BF16), struct((LINES, COLS), BF16)],
        in_specs=[SM, SM, SM, VM, VM, ANY, ANY],
        out_specs=[VM] * 5,
        scratch_shapes=[
            pltpu.VMEM((NODES, COLS), BF16),
            pltpu.VMEM((LINES * 16, NODES), BF16),
            pltpu.SemaphoreType.DMA((4,)),
            pltpu.SemaphoreType.DMA((LINES,)),
        ],
        compiler_params=params(),
        name="lines",
    )(place, nodes, admit, self_term, history, coupling, sources)

    from_near, from_sub, from_far = exchange(sub, near, far)

    packed, left, gathered, base = pl.pallas_call(
        functools.partial(terminals_kernel, capacity, slots),
        out_shape=[
            struct((slots * 4, LANES), F32),
            struct((slots, LANES), BF16),
            struct((LINES, LANES), BF16),
            struct((LINES, COLS), F32),
        ],
        in_specs=[SM, VM, VM, VM, VM, VM, VM, VM, ANY, ANY],
        out_specs=[VM] * 4,
        scratch_shapes=[
            pltpu.VMEM((NODES, SPANS * COLS), BF16),
            pltpu.VMEM((TERM_DEV + 2 * LINES, NODES), BF16),
            pltpu.SemaphoreType.DMA((8,)),
            pltpu.SemaphoreType.DMA,
        ],
        compiler_params=params(),
        name="terminals",
    )(
        nodes, self_term, rows, inj0, term_region.reshape(1, TERM_DEV),
        prior_phasor.reshape(TERM_DEV * 2, LANES), old_samples, tables, coupling, sources,
    )

    packed, sub, near, far, inj1 = pl.pallas_call(
        functools.partial(second_kernel, slots),
        out_shape=[
            struct((slots * 4, LANES), F32), block, block, block, struct((LINES, COLS), BF16)
        ],
        in_specs=[SM, SM, SM] + [VM] * 9,
        out_specs=[VM] * 5,
        input_output_aliases={11: 0},
        compiler_params=params(),
        name="second",
    )(
        place, nodes, admit, self_term, from_sub, from_near, from_far,
        base, gathered, left, tables[COLS:], packed,
    )

    result = lax.all_to_all(
        packed.reshape(region_count, capacity * 4, LANES),
        "region",
        split_axis=0,
        concat_axis=0,
        tiled=True,
    )
    phasors = result.reshape(slots, SPANS, 2, LANES)

    from_near, from_sub, from_far = exchange(sub, near, far)
    none = jnp.zeros_like(from_sub)
    next_history = jnp.stack(
        [
            jnp.where(odd_sub == 1, from_sub, none),
            jnp.where(odd_sub == 1, none, from_sub),
            jnp.where(odd_region == 1, from_near, from_far),
            jnp.where(odd_region == 1, from_far, from_near),
        ],
        axis=0,
    )[None]

    node_voltages = pl.pallas_call(
        nodes_kernel,
        grid=(NODES // ROWS,),
        out_shape=struct((1, NODES, SPANS * COLS), BF16),
        in_specs=[
            SM, VM, VM, VM,
            pl.BlockSpec((1, ROWS, NODES), lambda i: (0, i, 0)),
            pl.BlockSpec((1, NODES, SPANS * COLS), lambda i: (0, 0, 0), pipeline_mode=pl.Buffered(1)),
        ],
        out_specs=pl.BlockSpec((1, ROWS, SPANS * COLS), lambda i: (0, i, 0)),
        scratch_shapes=[
            pltpu.VMEM((NODES, LANES), BF16),
            pltpu.VMEM((LANES, SPANS * COLS), BF16),
        ],
        compiler_params=params(),
        cost_estimate=pl.CostEstimate(
            flops=2 * NODES * NODES * SPANS * COLS, bytes_accessed=20_000_000, transcendentals=0
        ),
        name="nodes",
    )(nodes, self_term, inj0, inj1, coupling, sources)
    return (next_history, node_voltages, phasors)


def solution(mesh):
    return jax.shard_map(
        body,
        mesh=mesh,
        in_specs=(
            P(("region", "sub"), None, None),
            P(("region", "sub"), None, None),
            P(("region", "sub"), None),
            P(("region", "sub"), None, None, None),
            P(("region", "sub"), None, None),
            P(("region", "sub"), None, None),
            P(("region", "sub"), None),
            P(("region", "sub"), None),
            P(("region", "sub"), None, None),
        ),
        out_specs=(
            P(("region", "sub"), None, None, None),
            P(("region", "sub"), None, None),
            P(("region", "sub"), None, None, None),
        ),
        check_vma=False,
    )
```

```python
import functools
import math

import jax
import jax.numpy as jnp
import numpy as np
from jax import lax
from jax.experimental import pallas as pl
from jax.experimental.pallas import tpu as pltpu
from jax.sharding import PartitionSpec as P

NODES = 2048
NEIGH = 4
LPP = 8
DELAY = 40
SPANS = 2
SCEN = 16
TERM_DEV = 256
BINS = 8
DFT_LEN = 2048

LINES = NEIGH * LPP
COLS = DELAY * SCEN
LANES = 128
PHASOR = 2 * BINS * SCEN
ROWS = 512
VMEM_LIMIT = 32 * 1024 * 1024

F32 = jnp.float32
BF16 = jnp.bfloat16


def fit_tables():
    step = np.arange(SPANS * DELAY)
    harmonic = np.arange(1, BINS + 1)
    angles = (step[:, None] * harmonic[None, :] % DFT_LEN) * (2.0 * math.pi / DFT_LEN)
    twiddle = np.stack([np.cos(angles), -np.sin(angles)], axis=1) / math.sqrt(DFT_LEN)
    table = np.einsum("uch,st->uscht", twiddle, np.eye(SCEN))
    table = table.reshape(SPANS, COLS, PHASOR).astype(np.float32)
    high = table.astype(jnp.bfloat16)
    low = (table - high.astype(np.float32)).astype(jnp.bfloat16)
    return np.concatenate([high, low, high], axis=1)


def dot(left, right):
    return jnp.dot(left, right, preferred_element_type=F32)


def split(value):
    high = value.astype(BF16)
    return high, (value - high.astype(F32)).astype(BF16)


def iota(shape, axis):
    return lax.broadcasted_iota(jnp.int32, shape, axis)


def slot_vectors(nodes_ref, admit_ref):
    lane = iota((1, LANES), 1)
    row_id = iota((LINES, 1), 0)
    along = jnp.full((1, LANES), -1, jnp.int32)
    down = jnp.full((LINES, 1), -1, jnp.int32)
    admit = jnp.zeros((LINES, 1), F32)
    for slot in range(LINES):
        node = nodes_ref[0, slot // LPP, slot % LPP]
        along = jnp.where((lane % LINES == slot) & (lane < 3 * LINES), node, along)
        down = jnp.where(row_id == slot, node, down)
        admit = jnp.where(row_id == slot, admit_ref[0, slot // LPP, slot % LPP], admit)
    return along, down, admit


def same_node(along, down):
    return (down == along) & (down >= 0)


def first_along(along, down):
    shape = (LINES, LANES)
    before = same_node(along, down) & (iota(shape, 0) < iota(shape, 1) % LINES)
    return (jnp.sum(jnp.where(before, 1, 0), axis=0, keepdims=True) == 0) & (along >= 0)


def first_down(along, down):
    shape = (LINES, LANES)
    before = same_node(along, down) & (iota(shape, 1) < iota(shape, 0))
    return (jnp.sum(jnp.where(before, 1, 0), axis=1, keepdims=True) == 0) & (down >= 0)


def injected(lines, along, down):
    pick = jnp.where(same_node(along, down), 1.0, 0.0).astype(BF16)[:, : 3 * LINES]
    high = lines.astype(BF16)
    mid, low = split(lines - high.astype(F32))
    total = dot(pick, jnp.concatenate([high, mid, low], axis=0)).astype(BF16)
    return total, jnp.where(first_down(along, down), total, jnp.zeros_like(total))


def three_times(rows):
    width = rows.shape[1]
    return jnp.concatenate([rows, rows, rows, jnp.zeros((LANES - 3 * LINES, width), rows.dtype)], axis=0)


def column_of(row):
    size = row.shape[1]
    eye = iota((size, size), 0) == iota((size, size), 1)
    return jnp.sum(jnp.where(eye, row, 0.0), axis=1, keepdims=True)


def small_left(gathered, self_col, along, first, offset):
    rows = gathered.shape[0]
    lane = iota((1, LANES), 1)
    high, low = split(self_col)
    here = (iota((rows, LANES), 0) + offset == along) & first & (lane >= LINES)
    weight = jnp.where(lane < 2 * LINES, high.astype(F32), low.astype(F32))
    return (gathered + jnp.where(here, weight, 0.0)).astype(BF16)


def send_out(volts, lines, admit, down, place_ref, sub_ref, near_ref, far_ref):
    outgoing = jnp.where(down >= 0, 2.0 * admit * volts - lines, 0.0)
    odd_region = place_ref[0] == 1
    odd_sub = place_ref[1] == 1
    lower_sub, upper_sub = outgoing[:LPP], outgoing[LPP : 2 * LPP]
    lower, upper = outgoing[2 * LPP : 3 * LPP], outgoing[3 * LPP :]
    sub_ref[...] = jnp.where(odd_sub, lower_sub, upper_sub)
    near_ref[...] = jnp.where(odd_region, lower, upper)
    far_ref[...] = jnp.where(odd_region, upper, lower)


def arrived(place_ref, from_sub_ref, from_near_ref, from_far_ref):
    odd_region = place_ref[0] == 1
    odd_sub = place_ref[1] == 1
    from_sub, near, far = from_sub_ref[...], from_near_ref[...], from_far_ref[...]
    none = jnp.zeros_like(from_sub)
    return jnp.concatenate(
        [
            jnp.where(odd_sub, from_sub, none),
            jnp.where(odd_sub, none, from_sub),
            jnp.where(odd_region, near, far),
            jnp.where(odd_region, far, near),
        ],
        axis=0,
    )


def lines_kernel(
    place_ref, nodes_hbm, admit_hbm, self_hbm, history_hbm, coupling_hbm, sources_hbm,
    sub_ref, near_ref, far_ref, src_ref, term_ref, rows_ref, gathered_ref, inj_ref,
    slot_ref, value_ref, self_ref,
    nodes_ref, admit_ref, history_ref, blocks, early_sem, src_sem, late_sem, block_sem,
):
    chunks = 2
    depth = NODES // chunks
    first_cols, later_cols = pl.ds(0, COLS), pl.ds(COLS, COLS)

    def early(index, source, target):
        return pltpu.make_async_copy(source, target, early_sem.at[index])

    def src_copy(part):
        rows = pl.ds(part * depth, depth)
        return pltpu.make_async_copy(
            sources_hbm.at[0, rows, first_cols], src_ref.at[rows, first_cols], src_sem.at[part]
        )

    def block_copy(slot):
        node = jnp.maximum(nodes_ref[0, slot // LPP, slot % LPP], 0)
        start = pl.multiple_of((node // 16) * 16, 16)
        return pltpu.make_async_copy(
            coupling_hbm.at[0, pl.ds(start, 16)], blocks.at[pl.ds(slot * 16, 16)], block_sem.at[slot]
        )

    nodes_copy = early(0, nodes_hbm, nodes_ref)
    admit_copy = early(1, admit_hbm, admit_ref)
    self_copy = early(2, self_hbm, self_ref)
    history_copy = early(3, history_hbm, history_ref)
    src_later = pltpu.make_async_copy(
        sources_hbm.at[0, :, later_cols], src_ref.at[:, later_cols], late_sem.at[0]
    )
    term_copy = pltpu.make_async_copy(
        coupling_hbm.at[0, pl.ds(0, TERM_DEV)], term_ref, late_sem.at[1]
    )
    nodes_copy.start()
    admit_copy.start()
    self_copy.start()
    history_copy.start()
    src_copy(0).start()
    nodes_copy.wait()
    for slot in range(LINES):
        block_copy(slot).start()
    for part in range(1, chunks):
        src_copy(part).start()
    admit_copy.wait()
    self_copy.wait()
    history_copy.wait()

    along, down, admit = slot_vectors(nodes_ref, admit_ref)
    lines = history_ref[0].reshape(LINES, COLS)
    total, injection = injected(lines, along, down)
    inj_ref[...] = injection
    at_node = jnp.maximum(down, 0)
    choose = jnp.where(
        iota((LINES, LINES * 16), 1) == iota((LINES, LINES * 16), 0) * 16 + at_node % 16, 1.0, 0.0
    ).astype(BF16)
    own_row = iota((LINES, NODES), 1) == at_node
    own = jnp.where(own_row, 1.0, 0.0).astype(BF16)
    self_col = jnp.sum(jnp.where(own_row, self_ref[...], 0.0), axis=1, keepdims=True)
    wanted = jnp.where(iota((1, LANES), 1) < LINES, along, -1)
    hot = jnp.where(iota((NODES, LANES), 0) == wanted, 1.0, 0.0).astype(BF16)
    src_ref[:, SPANS * COLS :] = hot
    slot_ref[:LINES, :] = jnp.broadcast_to(down, (LINES, LANES))
    slot_ref[LINES:, :] = jnp.broadcast_to(along, (8, LANES))
    value_ref[:LINES, :] = jnp.broadcast_to(admit, (LINES, LANES))
    value_ref[LINES:, :] = jnp.broadcast_to(self_col, (LINES, LANES))

    for slot in range(LINES):
        block_copy(slot).wait()
    term_copy.start()
    src_later.start()
    rows = dot(choose, blocks[...]).astype(BF16)
    rows_ref[...] = rows
    gathered = dot(rows, hot).astype(BF16)
    gathered_ref[...] = gathered
    volts = dot(gathered[:, :LINES], injection)
    left = jnp.concatenate([rows, own], axis=0)
    for part in range(chunks):
        src_copy(part).wait()
    picked = jnp.zeros((2 * LINES, COLS), F32)
    for part in range(chunks):
        span = slice(part * depth, (part + 1) * depth)
        picked = picked + dot(left[:, span], src_ref[span, :COLS])
    volts = volts + picked[:LINES] + self_col * (picked[LINES:] + total.astype(F32))
    send_out(volts, lines, admit, down, place_ref, sub_ref, near_ref, far_ref)
    src_later.wait()
    term_copy.wait()


def terminals_kernel(
    capacity, slots,
    slot_ref, inj_ref, src_ref, term_ref, self_ref, region_hbm, prior_hbm, old_hbm, table_hbm,
    packed_ref, left_ref, second_table,
    region_ref, prior_ref, old_ref, first_table, sems,
):
    copies = [
        pltpu.make_async_copy(source, target, sems.at[index])
        for index, (source, target) in enumerate(
            [
                (region_hbm, region_ref),
                (old_hbm, old_ref),
                (prior_hbm, prior_ref),
                (table_hbm.at[0], first_table),
                (table_hbm.at[1], second_table),
            ]
        )
    ]
    for copy in copies:
        copy.start()
    down = slot_ref[:LINES, :1]
    along = slot_ref[LINES : LINES + 1, :]
    first = first_along(along, down)
    term_self = column_of(self_ref[:, :TERM_DEV])

    sources = slice(0, SPANS * COLS)
    small = small_left(dot(term_ref[...], src_ref[:, SPANS * COLS :]), term_self, along, first, 0)
    volts = dot(term_ref[...], src_ref[:, sources])
    volts = volts + term_self * src_ref[:TERM_DEV, sources].astype(F32)
    from_lines = dot(small, three_times(inj_ref[...]))

    copies[0].wait()
    region_row = region_ref[...]
    region_col = column_of(region_row.astype(F32)).astype(jnp.int32)
    earlier = iota((TERM_DEV, TERM_DEV), 0) < iota((TERM_DEV, TERM_DEV), 1)
    rank = jnp.sum(
        jnp.where((region_col == region_row) & earlier, 1, 0), axis=0, keepdims=True
    )
    dest = region_row * capacity + rank
    pack = jnp.where(iota((slots, TERM_DEV), 0) == dest, 1.0, 0.0).astype(BF16)
    left_ref[...] = dot(pack, small).astype(BF16)

    for copy in copies[1:]:
        copy.wait()
    differences = volts - old_ref[...].astype(F32)
    running = jnp.concatenate(
        [prior_ref[pl.ds(part, TERM_DEV, stride=2), :] for part in range(2)], axis=1
    )
    highs, lows = [], []
    for span_index, table_ref in enumerate([first_table, second_table]):
        values = differences[:, span_index * COLS : (span_index + 1) * COLS]
        if span_index == 0:
            values = values + from_lines
        high, low = split(values)
        running = running + dot(jnp.concatenate([high, high, low], axis=1), table_ref[...])
        high, low = split(running)
        highs.append(high)
        lows.append(low)
    fitted = jnp.concatenate(
        [jnp.concatenate(highs, axis=1), jnp.concatenate(lows, axis=1)], axis=0
    )
    filled = dot(jnp.concatenate([pack, pack], axis=1), fitted)
    for part in range(4):
        packed_ref[pl.ds(part, slots, stride=4), :] = filled[:, part * LANES : (part + 1) * LANES]


def second_kernel(
    slots,
    place_ref, slot_ref, from_sub_ref, from_near_ref, from_far_ref, left_ref, table_ref, packed_in_ref,
    packed_ref,
):
    down = slot_ref[:LINES, :1]
    along = slot_ref[LINES : LINES + 1, :]
    lines = arrived(place_ref, from_sub_ref, from_near_ref, from_far_ref)
    _, injection = injected(lines, along, down)
    spectrum = dot(jnp.concatenate([injection, injection], axis=1), table_ref[: 2 * COLS, :])
    high, low = split(spectrum)
    left = left_ref[...]
    change = dot(
        jnp.concatenate([left, left], axis=1),
        jnp.concatenate([three_times(high), three_times(low)], axis=0),
    )
    for row in range(2):
        rows = pl.ds(row, slots, stride=4)
        packed_ref[rows, :] = packed_in_ref[rows, :]
    for part in range(2):
        rows = pl.ds(2 + part, slots, stride=4)
        packed_ref[rows, :] = packed_in_ref[rows, :] + change[:, part * LANES : (part + 1) * LANES]


def last_lines_kernel(
    place_ref, slot_ref, value_ref, from_sub_ref, from_near_ref, from_far_ref,
    rows_ref, gathered_ref, src_ref, started_ref,
    sub_ref, near_ref, far_ref, inj_ref,
):
    del started_ref
    down = slot_ref[:LINES, :1]
    along = slot_ref[LINES : LINES + 1, :]
    admit, self_col = value_ref[:LINES, :1], value_ref[LINES:, :1]
    lines = arrived(place_ref, from_sub_ref, from_near_ref, from_far_ref)
    total, injection = injected(lines, along, down)
    inj_ref[...] = injection
    own = jnp.where(iota((LINES, NODES), 1) == jnp.maximum(down, 0), 1.0, 0.0).astype(BF16)
    left = jnp.concatenate([rows_ref[...], own], axis=0)
    picked = dot(left, src_ref[:, COLS : SPANS * COLS])
    volts = picked[:LINES] + dot(gathered_ref[:, :LINES], injection)
    volts = volts + self_col * (picked[LINES:] + total.astype(F32))
    send_out(volts, lines, admit, down, place_ref, sub_ref, near_ref, far_ref)


def nodes_kernel(
    slot_ref, inj0_ref, inj1_ref, src_ref, self_ref, coupling_hbm,
    volts_hbm,
    matrix_buf, volts_buf, small_buf, in_sem, out_sem,
):
    down = slot_ref[:LINES, :1]
    along = slot_ref[LINES : LINES + 1, :]
    first = first_along(along, down)
    blocks = NODES // ROWS

    def load(block, place):
        rows = pl.ds(pl.multiple_of(block * ROWS, ROWS), ROWS)
        return pltpu.make_async_copy(coupling_hbm.at[0, rows], matrix_buf.at[place], in_sem.at[place])

    def store(block, place):
        rows = pl.ds(pl.multiple_of(block * ROWS, ROWS), ROWS)
        return pltpu.make_async_copy(volts_buf.at[place], volts_hbm.at[0, rows], out_sem.at[place])

    load(0, 0).start()
    small_buf[...] = three_times(jnp.concatenate([inj0_ref[...], inj1_ref[...]], axis=1))

    @pl.loop(0, blocks)
    def _(block):
        place = lax.rem(block, 2)

        @pl.when(block + 1 < blocks)
        def _():
            load(block + 1, 1 - place).start()

        load(block, place).wait()

        @pl.when(block >= 2)
        def _():
            store(block - 2, place).wait()

        start = pl.multiple_of(block * ROWS, ROWS)
        matrix = matrix_buf[place]
        self_col = jnp.concatenate(
            [
                column_of(self_ref[:, pl.ds(pl.multiple_of(start + part, 256), 256)])
                for part in range(0, ROWS, 256)
            ],
            axis=0,
        )
        products = dot(matrix, src_ref[...])
        small = small_left(products[:, SPANS * COLS :], self_col, along, first, start)
        total = products[:, : SPANS * COLS] + dot(small, small_buf[...])
        total = total + self_col * src_ref[pl.ds(start, ROWS), : SPANS * COLS].astype(F32)
        volts_buf[place] = total.astype(BF16)
        store(block, place).start()

    for block in range(blocks - 2, blocks):
        store(block, block % 2).wait()


VM = pl.BlockSpec(memory_space=pltpu.VMEM)
SM = pl.BlockSpec(memory_space=pltpu.SMEM)
HB = pl.BlockSpec(memory_space=pltpu.HBM)


def struct(shape, dtype):
    return jax.ShapeDtypeStruct(shape, dtype)


def in_hbm(*arrays):
    return [pltpu.with_memory_space_constraint(array, pltpu.HBM) for array in arrays]


def in_vmem(*arrays):
    return [pltpu.with_memory_space_constraint(array, pltpu.VMEM) for array in arrays]


def params():
    return pltpu.CompilerParams(vmem_limit_bytes=VMEM_LIMIT)


def exchange(sub, near, far):
    subs = lax.axis_size("sub")
    regions = lax.axis_size("region")

    def swap(block, axis, size, first):
        pairs = []
        for low in range(first, size - 1, 2):
            pairs += [(low, low + 1), (low + 1, low)]
        return lax.ppermute(block, axis, pairs)

    return (
        swap(near, "region", regions, 0),
        swap(sub, "sub", subs, 0),
        swap(far, "region", regions, 1),
    )


def body(
    sources,
    coupling,
    self_term,
    history,
    line_nodes,
    line_admit,
    term_region,
    old_samples,
    prior_phasor,
):
    region_count = lax.axis_size("region")
    capacity = max(2, 2 * TERM_DEV // region_count)
    slots = region_count * capacity
    odd_region = lax.axis_index("region") % 2
    odd_sub = lax.axis_index("sub") % 2
    place = jnp.stack([odd_region, odd_sub]).astype(jnp.int32)
    block = struct((LPP, COLS), F32)
    injection = struct((LINES, COLS), BF16)
    tables = fit_tables()
    DMA = pltpu.SemaphoreType.DMA

    (sub, near, far, src, term, rows, gathered, inj0, slot, value, self_row) = pl.pallas_call(
        lines_kernel,
        out_shape=[
            block, block, block,
            struct((NODES, SPANS * COLS + LANES), BF16),
            struct((TERM_DEV, NODES), BF16),
            struct((LINES, NODES), BF16),
            struct((LINES, LANES), BF16),
            injection,
            struct((LINES + 8, LANES), jnp.int32),
            struct((2 * LINES, LANES), F32),
            struct((1, NODES), F32),
        ],
        in_specs=[SM] + [HB] * 6,
        out_specs=[VM] * 11,
        scratch_shapes=[
            pltpu.SMEM((1, NEIGH, LPP), jnp.int32),
            pltpu.SMEM((1, NEIGH, LPP), F32),
            pltpu.VMEM((1, NEIGH, LPP, COLS), F32),
            pltpu.VMEM((LINES * 16, NODES), BF16),
            DMA((4,)), DMA((2,)), DMA((2,)), DMA((LINES,)),
        ],
        compiler_params=params(),
        name="lines",
    )(place, *in_hbm(line_nodes, line_admit, self_term, history, coupling, sources))

    from_near, from_sub, from_far = exchange(sub, near, far)

    packed, left, table = pl.pallas_call(
        functools.partial(terminals_kernel, capacity, slots),
        out_shape=[
            struct((slots * 4, LANES), F32),
            struct((slots, LANES), BF16),
            struct((3 * COLS, PHASOR), BF16),
        ],
        in_specs=[VM] * 5 + [HB] * 4,
        out_specs=[VM] * 3,
        scratch_shapes=[
            pltpu.VMEM((1, TERM_DEV), jnp.int32),
            pltpu.VMEM((TERM_DEV * 2, LANES), F32),
            pltpu.VMEM((TERM_DEV, SPANS * COLS), BF16),
            pltpu.VMEM((3 * COLS, PHASOR), BF16),
            DMA((5,)),
        ],
        compiler_params=params(),
        name="terminals",
    )(
        slot, inj0, src, term, self_row,
        *in_hbm(
            term_region.reshape(1, TERM_DEV),
            prior_phasor.reshape(TERM_DEV * 2, LANES),
            old_samples,
            jnp.asarray(tables),
        ),
    )

    packed = pl.pallas_call(
        functools.partial(second_kernel, slots),
        out_shape=struct((slots * 4, LANES), F32),
        in_specs=[SM] + [VM] * 7,
        out_specs=VM,
        compiler_params=params(),
        name="second",
    )(place, slot, from_sub, from_near, from_far, left, table, packed)

    result = lax.all_to_all(
        packed.reshape(region_count, capacity * 4, LANES),
        "region",
        split_axis=0,
        concat_axis=0,
        tiled=True,
    )
    phasors = result.reshape(slots, SPANS, 2, LANES)

    sub, near, far, inj1 = pl.pallas_call(
        last_lines_kernel,
        out_shape=[block, block, block, injection],
        in_specs=[SM] + [VM] * 8 + [pl.BlockSpec(memory_space=pl.ANY)],
        out_specs=[VM] * 4,
        compiler_params=params(),
        name="last_lines",
    )(place, slot, value, from_sub, from_near, from_far, rows, gathered, src, packed)

    from_near, from_sub, from_far = exchange(sub, near, far)
    none = jnp.zeros_like(from_sub)
    next_history = jnp.stack(
        [
            jnp.where(odd_sub == 1, from_sub, none),
            jnp.where(odd_sub == 1, none, from_sub),
            jnp.where(odd_region == 1, from_near, from_far),
            jnp.where(odd_region == 1, from_far, from_near),
        ],
        axis=0,
    )[None]

    node_voltages = pl.pallas_call(
        nodes_kernel,
        out_shape=struct((1, NODES, SPANS * COLS), BF16),
        in_specs=[VM] * 5 + [HB],
        out_specs=HB,
        scratch_shapes=[
            pltpu.VMEM((2, ROWS, NODES), BF16),
            pltpu.VMEM((2, ROWS, SPANS * COLS), BF16),
            pltpu.VMEM((LANES, SPANS * COLS), BF16),
            DMA((2,)), DMA((2,)),
        ],
        compiler_params=params(),
        cost_estimate=pl.CostEstimate(
            flops=2 * NODES * NODES * SPANS * COLS, bytes_accessed=20_000_000, transcendentals=0
        ),
        name="nodes",
    )(slot, inj0, inj1, src, self_row, *in_hbm(coupling))
    return (next_history, node_voltages, phasors)


def solution(mesh):
    return jax.shard_map(
        body,
        mesh=mesh,
        in_specs=(
            P(("region", "sub"), None, None),
            P(("region", "sub"), None, None),
            P(("region", "sub"), None),
            P(("region", "sub"), None, None, None),
            P(("region", "sub"), None, None),
            P(("region", "sub"), None, None),
            P(("region", "sub"), None),
            P(("region", "sub"), None),
            P(("region", "sub"), None, None),
        ),
        out_specs=(
            P(("region", "sub"), None, None, None),
            P(("region", "sub"), None, None),
            P(("region", "sub"), None, None, None),
        ),
        check_vma=False,
    )
```

```python
import functools
import math

import jax
import jax.numpy as jnp
import numpy as np
from jax import lax
from jax.experimental import pallas as pl
from jax.experimental.pallas import tpu as pltpu
from jax.sharding import PartitionSpec as P

NODES = 2048
NEIGH = 4
LPP = 8
DELAY = 40
SPANS = 2
SCEN = 16
TERM_DEV = 256
BINS = 8
DFT_LEN = 2048

LINES = NEIGH * LPP
COLS = DELAY * SCEN
LANES = 128
PHASOR = 2 * BINS * SCEN
ROWS = 512
VMEM_LIMIT = 32 * 1024 * 1024

F32 = jnp.float32
BF16 = jnp.bfloat16


def fit_table():
    step = np.arange(DELAY)
    harmonic = np.arange(1, BINS + 1)
    angles = (step[:, None] * harmonic[None, :] % DFT_LEN) * (2.0 * math.pi / DFT_LEN)
    twiddle = np.stack([np.cos(angles), -np.sin(angles)], axis=1) / math.sqrt(DFT_LEN)
    table = np.einsum("uch,st->uscht", twiddle, np.eye(SCEN))
    table = table.reshape(COLS, PHASOR).astype(np.float32)
    high = table.astype(jnp.bfloat16)
    low = (table - high.astype(np.float32)).astype(jnp.bfloat16)
    return np.concatenate([high, low], axis=1)


def fit(values, table_ref):
    high, low = split(values)
    both = dot(high, table_ref[...])
    return both[:, :PHASOR] + both[:, PHASOR:] + dot(low, table_ref[:, :PHASOR])


def span_turn():
    angles = 2.0 * math.pi / DFT_LEN * DELAY * np.repeat(np.arange(1, BINS + 1), SCEN)
    return np.stack([np.cos(angles), np.sin(angles)] * 4).astype(np.float32)


def turned(values, turn_ref):
    cosine, sine = turn_ref[0:1, :], turn_ref[1:2, :]
    real, imag = values[:, :LANES], values[:, LANES:]
    return jnp.concatenate([real * cosine + imag * sine, imag * cosine - real * sine], axis=1)


def dot(left, right):
    return jnp.dot(left, right, preferred_element_type=F32)


def split(value):
    high = value.astype(BF16)
    return high, (value - high.astype(F32)).astype(BF16)


def iota(shape, axis):
    return lax.broadcasted_iota(jnp.int32, shape, axis)


def slot_vectors(nodes_ref, admit_ref):
    lane = iota((1, LANES), 1)
    row_id = iota((LINES, 1), 0)
    along = jnp.full((1, LANES), -1, jnp.int32)
    down = jnp.full((LINES, 1), -1, jnp.int32)
    admit = jnp.zeros((LINES, 1), F32)
    for slot in range(LINES):
        node = nodes_ref[0, slot // LPP, slot % LPP]
        along = jnp.where((lane % LINES == slot) & (lane < 3 * LINES), node, along)
        down = jnp.where(row_id == slot, node, down)
        admit = jnp.where(row_id == slot, admit_ref[0, slot // LPP, slot % LPP], admit)
    return along, down, admit


def same_node(along, down):
    return (down == along) & (down >= 0)


def first_along(along, down):
    shape = (LINES, LANES)
    before = same_node(along, down) & (iota(shape, 0) < iota(shape, 1) % LINES)
    return (jnp.sum(jnp.where(before, 1, 0), axis=0, keepdims=True) == 0) & (along >= 0)


def first_down(along, down):
    shape = (LINES, LANES)
    before = same_node(along, down) & (iota(shape, 1) < iota(shape, 0))
    return (jnp.sum(jnp.where(before, 1, 0), axis=1, keepdims=True) == 0) & (down >= 0)


def injected(lines, along, down):
    pick = jnp.where(same_node(along, down), 1.0, 0.0).astype(BF16)[:, : 3 * LINES]
    high = lines.astype(BF16)
    mid, low = split(lines - high.astype(F32))
    total = dot(pick, jnp.concatenate([high, mid, low], axis=0)).astype(BF16)
    return total, jnp.where(first_down(along, down), total, jnp.zeros_like(total))


def three_times(rows):
    width = rows.shape[1]
    return jnp.concatenate([rows, rows, rows, jnp.zeros((LANES - 3 * LINES, width), rows.dtype)], axis=0)


def column_of(row):
    size = row.shape[1]
    eye = iota((size, size), 0) == iota((size, size), 1)
    return jnp.sum(jnp.where(eye, row, 0.0), axis=1, keepdims=True)


def small_left(gathered, self_col, along, first, offset):
    rows = gathered.shape[0]
    lane = iota((1, LANES), 1)
    high, low = split(self_col)
    here = (iota((rows, LANES), 0) + offset == along) & first & (lane >= LINES)
    weight = jnp.where(lane < 2 * LINES, high.astype(F32), low.astype(F32))
    return (gathered + jnp.where(here, weight, 0.0)).astype(BF16)


def send_out(volts, lines, admit, down, place_ref, sub_ref, near_ref, far_ref):
    outgoing = jnp.where(down >= 0, 2.0 * admit * volts - lines, 0.0)
    odd_region = place_ref[0] == 1
    odd_sub = place_ref[1] == 1
    lower_sub, upper_sub = outgoing[:LPP], outgoing[LPP : 2 * LPP]
    lower, upper = outgoing[2 * LPP : 3 * LPP], outgoing[3 * LPP :]
    sub_ref[...] = jnp.where(odd_sub, lower_sub, upper_sub)
    near_ref[...] = jnp.where(odd_region, lower, upper)
    far_ref[...] = jnp.where(odd_region, upper, lower)


def arrived(place_ref, from_sub_ref, from_near_ref, from_far_ref):
    odd_region = place_ref[0] == 1
    odd_sub = place_ref[1] == 1
    from_sub, near, far = from_sub_ref[...], from_near_ref[...], from_far_ref[...]
    none = jnp.zeros_like(from_sub)
    return jnp.concatenate(
        [
            jnp.where(odd_sub, from_sub, none),
            jnp.where(odd_sub, none, from_sub),
            jnp.where(odd_region, near, far),
            jnp.where(odd_region, far, near),
        ],
        axis=0,
    )


def lines_kernel(
    place_ref, nodes_hbm, admit_hbm, self_hbm, history_hbm, coupling_hbm, sources_hbm,
    region_hbm, prior_hbm, old_hbm, table_hbm, turn_hbm,
    sub_ref, near_ref, far_ref, src_ref, term_ref, rows_ref, gathered_ref, inj_ref,
    slot_ref, value_ref, self_ref, region_ref, prior_ref, old_ref, table_ref, turn_ref,
    nodes_ref, admit_ref, history_ref, blocks, early_sem, src_sem, late_sem, block_sem,
):
    chunks = 2
    depth = NODES // chunks
    first_cols = pl.ds(0, COLS)

    def early(index, source, target):
        return pltpu.make_async_copy(source, target, early_sem.at[index])

    def src_copy(part):
        rows = pl.ds(part * depth, depth)
        return pltpu.make_async_copy(
            sources_hbm.at[0, rows, first_cols], src_ref.at[rows, first_cols], src_sem.at[part]
        )

    def block_copy(slot):
        node = jnp.maximum(nodes_ref[0, slot // LPP, slot % LPP], 0)
        start = pl.multiple_of((node // 16) * 16, 16)
        return pltpu.make_async_copy(
            coupling_hbm.at[0, pl.ds(start, 16)], blocks.at[pl.ds(slot * 16, 16)], block_sem.at[slot]
        )

    nodes_copy = early(0, nodes_hbm, nodes_ref)
    admit_copy = early(1, admit_hbm, admit_ref)
    self_copy = early(2, self_hbm, self_ref)
    history_copy = early(3, history_hbm, history_ref)
    late_copies = [
        pltpu.make_async_copy(source, target, late_sem.at[index])
        for index, (source, target) in enumerate(
            [
                (coupling_hbm.at[0, pl.ds(0, TERM_DEV)], term_ref),
                (region_hbm, region_ref),
                (prior_hbm, prior_ref),
                (old_hbm, old_ref),
                (table_hbm, table_ref),
                (turn_hbm, turn_ref),
            ]
        )
    ]
    nodes_copy.start()
    admit_copy.start()
    self_copy.start()
    history_copy.start()
    for part in range(chunks):
        src_copy(part).start()
    nodes_copy.wait()
    for slot in range(LINES):
        block_copy(slot).start()
    admit_copy.wait()
    self_copy.wait()
    history_copy.wait()

    along, down, admit = slot_vectors(nodes_ref, admit_ref)
    lines = history_ref[0].reshape(LINES, COLS)
    total, injection = injected(lines, along, down)
    inj_ref[...] = injection
    at_node = jnp.maximum(down, 0)
    choose = jnp.where(
        iota((LINES, LINES * 16), 1) == iota((LINES, LINES * 16), 0) * 16 + at_node % 16, 1.0, 0.0
    ).astype(BF16)
    own_row = iota((LINES, NODES), 1) == at_node
    own = jnp.where(own_row, 1.0, 0.0).astype(BF16)
    self_col = jnp.sum(jnp.where(own_row, self_ref[...], 0.0), axis=1, keepdims=True)
    wanted = jnp.where(iota((1, LANES), 1) < LINES, along, -1)
    hot = jnp.where(iota((NODES, LANES), 0) == wanted, 1.0, 0.0).astype(BF16)
    src_ref[:, COLS:] = hot
    slot_ref[:LINES, :] = jnp.broadcast_to(down, (LINES, LANES))
    slot_ref[LINES:, :] = jnp.broadcast_to(along, (8, LANES))
    value_ref[:LINES, :] = jnp.broadcast_to(admit, (LINES, LANES))
    value_ref[LINES:, :] = jnp.broadcast_to(self_col, (LINES, LANES))

    for slot in range(LINES):
        block_copy(slot).wait()
    for copy in late_copies:
        copy.start()
    rows = dot(choose, blocks[...]).astype(BF16)
    rows_ref[...] = rows
    gathered = dot(rows, hot).astype(BF16)
    gathered_ref[...] = gathered
    volts = dot(gathered[:, :LINES], injection)
    left = jnp.concatenate([rows, own], axis=0)
    for part in range(chunks):
        src_copy(part).wait()
    picked = jnp.zeros((2 * LINES, COLS), F32)
    for part in range(chunks):
        span = slice(part * depth, (part + 1) * depth)
        picked = picked + dot(left[:, span], src_ref[span, :COLS])
    volts = volts + picked[:LINES] + self_col * (picked[LINES:] + total.astype(F32))
    send_out(volts, lines, admit, down, place_ref, sub_ref, near_ref, far_ref)
    for copy in late_copies:
        copy.wait()


def terminals_kernel(
    capacity, slots,
    slot_ref, inj_ref, src_ref, term_ref, self_ref, region_ref, prior_ref, old_ref, table_ref, turn_ref,
    sources_hbm,
    packed_ref, left_ref,
    later_ref, later_sem,
):
    later_copy = pltpu.make_async_copy(sources_hbm.at[0, :, pl.ds(COLS, COLS)], later_ref, later_sem)
    later_copy.start()
    down = slot_ref[:LINES, :1]
    along = slot_ref[LINES : LINES + 1, :]
    first = first_along(along, down)
    term_self = column_of(self_ref[:, :TERM_DEV])

    products = dot(term_ref[...], src_ref[...])
    small = small_left(products[:, COLS:], term_self, along, first, 0)
    volts = products[:, :COLS] + term_self * src_ref[:TERM_DEV, :COLS].astype(F32)
    volts = volts + dot(small, three_times(inj_ref[...]))

    region_row = region_ref[...]
    region_col = column_of(region_row.astype(F32)).astype(jnp.int32)
    earlier = iota((TERM_DEV, TERM_DEV), 0) < iota((TERM_DEV, TERM_DEV), 1)
    rank = jnp.sum(
        jnp.where((region_col == region_row) & earlier, 1, 0), axis=0, keepdims=True
    )
    dest = region_row * capacity + rank
    pack = jnp.where(iota((slots, TERM_DEV), 0) == dest, 1.0, 0.0).astype(BF16)
    left_ref[...] = dot(pack, small).astype(BF16)

    doubled = jnp.concatenate([pack, pack], axis=1)

    def put(span_index, running):
        filled = dot(doubled, jnp.concatenate(split(running), axis=0))
        for part in range(2):
            packed_ref[pl.ds(2 * span_index + part, slots, stride=4), :] = filled[
                :, part * LANES : (part + 1) * LANES
            ]

    running = jnp.concatenate(
        [prior_ref[pl.ds(part, TERM_DEV, stride=2), :] for part in range(2)], axis=1
    )
    running = running + fit(volts - old_ref[:, :COLS].astype(F32), table_ref)
    put(0, running)
    later_copy.wait()
    volts = dot(term_ref[...], later_ref[...]) + term_self * later_ref[:TERM_DEV, :].astype(F32)
    put(1, running + turned(fit(volts - old_ref[:, COLS:].astype(F32), table_ref), turn_ref))


def second_kernel(
    slots,
    place_ref, slot_ref, from_sub_ref, from_near_ref, from_far_ref, left_ref, table_ref, turn_ref, packed_in_ref,
    packed_ref,
):
    down = slot_ref[:LINES, :1]
    along = slot_ref[LINES : LINES + 1, :]
    lines = arrived(place_ref, from_sub_ref, from_near_ref, from_far_ref)
    _, injection = injected(lines, along, down)
    both = dot(injection, table_ref[...])
    high, low = split(turned(both[:, :PHASOR] + both[:, PHASOR:], turn_ref))
    left = left_ref[...]
    change = dot(
        jnp.concatenate([left, left], axis=1),
        jnp.concatenate([three_times(high), three_times(low)], axis=0),
    )
    for row in range(2):
        rows = pl.ds(row, slots, stride=4)
        packed_ref[rows, :] = packed_in_ref[rows, :]
    for part in range(2):
        rows = pl.ds(2 + part, slots, stride=4)
        packed_ref[rows, :] = packed_in_ref[rows, :] + change[:, part * LANES : (part + 1) * LANES]


def last_lines_kernel(
    place_ref, slot_ref, value_ref, from_sub_ref, from_near_ref, from_far_ref,
    rows_ref, gathered_ref, sources_hbm, started_ref,
    sub_ref, near_ref, far_ref, inj_ref,
    src_ref, sems,
):
    del started_ref
    chunks = 2
    depth = NODES // chunks
    copies = [
        pltpu.make_async_copy(
            sources_hbm.at[0, pl.ds(part * depth, depth), pl.ds(COLS, COLS)],
            src_ref.at[pl.ds(part * depth, depth)],
            sems.at[part],
        )
        for part in range(chunks)
    ]
    for copy in copies:
        copy.start()
    down = slot_ref[:LINES, :1]
    along = slot_ref[LINES : LINES + 1, :]
    admit, self_col = value_ref[:LINES, :1], value_ref[LINES:, :1]
    lines = arrived(place_ref, from_sub_ref, from_near_ref, from_far_ref)
    total, injection = injected(lines, along, down)
    inj_ref[...] = injection
    own = jnp.where(iota((LINES, NODES), 1) == jnp.maximum(down, 0), 1.0, 0.0).astype(BF16)
    left = jnp.concatenate([rows_ref[...], own], axis=0)
    volts = dot(gathered_ref[:, :LINES], injection)
    picked = jnp.zeros((2 * LINES, COLS), F32)
    for part in range(chunks):
        copies[part].wait()
        span = slice(part * depth, (part + 1) * depth)
        picked = picked + dot(left[:, span], src_ref[span, :])
    volts = volts + picked[:LINES] + self_col * (picked[LINES:] + total.astype(F32))
    send_out(volts, lines, admit, down, place_ref, sub_ref, near_ref, far_ref)


def nodes_kernel(
    inj0_ref, inj1_ref, self_ref, nodes_hbm, sources_hbm, coupling_hbm,
    volts_hbm,
    nodes_ref, drive_ref, matrix_buf, volts_buf, early_sem, in_sem, out_sem,
):
    blocks = NODES // ROWS

    def load(block, place):
        rows = pl.ds(pl.multiple_of(block * ROWS, ROWS), ROWS)
        return pltpu.make_async_copy(coupling_hbm.at[0, rows], matrix_buf.at[place], in_sem.at[place])

    def store(block, place):
        rows = pl.ds(pl.multiple_of(block * ROWS, ROWS), ROWS)
        return pltpu.make_async_copy(volts_buf.at[place], volts_hbm.at[0, rows], out_sem.at[place])

    nodes_copy = pltpu.make_async_copy(nodes_hbm, nodes_ref, early_sem.at[0])
    drive_copy = pltpu.make_async_copy(sources_hbm.at[0], drive_ref, early_sem.at[1])
    nodes_copy.start()
    drive_copy.start()
    load(0, 0).start()
    nodes_copy.wait()
    drive_copy.wait()

    both = jnp.concatenate([inj0_ref[...], inj1_ref[...]], axis=1).astype(F32)
    for slot in range(LINES):
        node = jnp.maximum(nodes_ref[0, slot // LPP, slot % LPP], 0)
        rows = pl.ds(pl.multiple_of((node // 16) * 16, 16), 16)
        extra = jnp.where(iota((16, 1), 0) == node % 16, both[slot : slot + 1, :], 0.0)
        drive_ref[rows, :] = (drive_ref[rows, :].astype(F32) + extra).astype(BF16)

    @pl.loop(0, blocks)
    def _(block):
        place = lax.rem(block, 2)

        @pl.when(block + 1 < blocks)
        def _():
            load(block + 1, 1 - place).start()

        load(block, place).wait()

        @pl.when(block >= 2)
        def _():
            store(block - 2, place).wait()

        start = pl.multiple_of(block * ROWS, ROWS)
        block_self = jnp.concatenate(
            [
                column_of(self_ref[:, pl.ds(pl.multiple_of(start + part, 256), 256)])
                for part in range(0, ROWS, 256)
            ],
            axis=0,
        )
        result = dot(matrix_buf[place], drive_ref[...])
        result = result + block_self * drive_ref[pl.ds(start, ROWS), :].astype(F32)
        volts_buf[place] = result.astype(BF16)
        store(block, place).start()

    for block in range(blocks - 2, blocks):
        store(block, block % 2).wait()


VM = pl.BlockSpec(memory_space=pltpu.VMEM)
SM = pl.BlockSpec(memory_space=pltpu.SMEM)
HB = pl.BlockSpec(memory_space=pltpu.HBM)


def struct(shape, dtype):
    return jax.ShapeDtypeStruct(shape, dtype)


def in_hbm(*arrays):
    return [pltpu.with_memory_space_constraint(array, pltpu.HBM) for array in arrays]


def in_vmem(*arrays):
    return [pltpu.with_memory_space_constraint(array, pltpu.VMEM) for array in arrays]


def params():
    return pltpu.CompilerParams(vmem_limit_bytes=VMEM_LIMIT)


def exchange(sub, near, far):
    subs = lax.axis_size("sub")
    regions = lax.axis_size("region")

    def swap(block, axis, size, first):
        pairs = []
        for low in range(first, size - 1, 2):
            pairs += [(low, low + 1), (low + 1, low)]
        return lax.ppermute(block, axis, pairs)

    return (
        swap(near, "region", regions, 0),
        swap(sub, "sub", subs, 0),
        swap(far, "region", regions, 1),
    )


def body(
    sources,
    coupling,
    self_term,
    history,
    line_nodes,
    line_admit,
    term_region,
    old_samples,
    prior_phasor,
):
    region_count = lax.axis_size("region")
    capacity = max(2, 2 * TERM_DEV // region_count)
    slots = region_count * capacity
    odd_region = lax.axis_index("region") % 2
    odd_sub = lax.axis_index("sub") % 2
    place = jnp.stack([odd_region, odd_sub]).astype(jnp.int32)
    block = struct((LPP, COLS), F32)
    injection = struct((LINES, COLS), BF16)
    DMA = pltpu.SemaphoreType.DMA

    (
        sub, near, far, src, term, rows, gathered, inj0, slot, value, self_row,
        region, prior, old, table, turn,
    ) = pl.pallas_call(
        lines_kernel,
        out_shape=[
            block, block, block,
            struct((NODES, COLS + LANES), BF16),
            struct((TERM_DEV, NODES), BF16),
            struct((LINES, NODES), BF16),
            struct((LINES, LANES), BF16),
            injection,
            struct((LINES + 8, LANES), jnp.int32),
            struct((2 * LINES, LANES), F32),
            struct((1, NODES), F32),
            struct((1, TERM_DEV), jnp.int32),
            struct((TERM_DEV * 2, LANES), F32),
            struct((TERM_DEV, SPANS * COLS), BF16),
            struct((COLS, 2 * PHASOR), BF16),
            struct((8, LANES), F32),
        ],
        in_specs=[SM] + [HB] * 11,
        out_specs=[VM] * 16,
        scratch_shapes=[
            pltpu.SMEM((1, NEIGH, LPP), jnp.int32),
            pltpu.SMEM((1, NEIGH, LPP), F32),
            pltpu.VMEM((1, NEIGH, LPP, COLS), F32),
            pltpu.VMEM((LINES * 16, NODES), BF16),
            DMA((4,)), DMA((2,)), DMA((6,)), DMA((LINES,)),
        ],
        compiler_params=params(),
        name="lines",
    )(
        place,
        *in_hbm(
            line_nodes, line_admit, self_term, history, coupling, sources,
            term_region.reshape(1, TERM_DEV), prior_phasor.reshape(TERM_DEV * 2, LANES), old_samples,
            jnp.asarray(fit_table()), jnp.asarray(span_turn()),
        ),
    )

    from_near, from_sub, from_far = exchange(sub, near, far)

    packed, left = pl.pallas_call(
        functools.partial(terminals_kernel, capacity, slots),
        out_shape=[struct((slots * 4, LANES), F32), struct((slots, LANES), BF16)],
        in_specs=[VM] * 10 + [HB],
        out_specs=[VM] * 2,
        scratch_shapes=[pltpu.VMEM((NODES, COLS), BF16), DMA],
        compiler_params=params(),
        name="terminals",
    )(slot, inj0, src, term, self_row, region, prior, old, table, turn, *in_hbm(sources))

    packed = pl.pallas_call(
        functools.partial(second_kernel, slots),
        out_shape=struct((slots * 4, LANES), F32),
        in_specs=[SM] + [VM] * 8,
        out_specs=VM,
        compiler_params=params(),
        name="second",
    )(place, slot, from_sub, from_near, from_far, left, table, turn, packed)

    result = lax.all_to_all(
        packed.reshape(region_count, capacity * 4, LANES),
        "region",
        split_axis=0,
        concat_axis=0,
        tiled=True,
    )
    phasors = result.reshape(slots, SPANS, 2, LANES)

    sub, near, far, inj1 = pl.pallas_call(
        last_lines_kernel,
        out_shape=[block, block, block, injection],
        in_specs=[SM] + [VM] * 7 + [HB, pl.BlockSpec(memory_space=pl.ANY)],
        out_specs=[VM] * 4,
        scratch_shapes=[pltpu.VMEM((NODES, COLS), BF16), DMA((2,))],
        compiler_params=params(),
        name="last_lines",
    )(
        place, slot, value, from_sub, from_near, from_far, rows, gathered,
        *in_hbm(sources), packed,
    )

    from_near, from_sub, from_far = exchange(sub, near, far)
    none = jnp.zeros_like(from_sub)
    next_history = jnp.stack(
        [
            jnp.where(odd_sub == 1, from_sub, none),
            jnp.where(odd_sub == 1, none, from_sub),
            jnp.where(odd_region == 1, from_near, from_far),
            jnp.where(odd_region == 1, from_far, from_near),
        ],
        axis=0,
    )[None]

    node_voltages = pl.pallas_call(
        nodes_kernel,
        out_shape=struct((1, NODES, SPANS * COLS), BF16),
        in_specs=[VM] * 3 + [HB] * 3,
        out_specs=HB,
        scratch_shapes=[
            pltpu.SMEM((1, NEIGH, LPP), jnp.int32),
            pltpu.VMEM((NODES, SPANS * COLS), BF16),
            pltpu.VMEM((2, ROWS, NODES), BF16),
            pltpu.VMEM((2, ROWS, SPANS * COLS), BF16),
            DMA((2,)), DMA((2,)), DMA((2,)),
        ],
        compiler_params=params(),
        cost_estimate=pl.CostEstimate(
            flops=2 * NODES * NODES * SPANS * COLS, bytes_accessed=20_000_000, transcendentals=0
        ),
        name="nodes",
    )(inj0, inj1, self_row, *in_hbm(line_nodes, sources, coupling))
    return (next_history, node_voltages, phasors)


def solution(mesh):
    return jax.shard_map(
        body,
        mesh=mesh,
        in_specs=(
            P(("region", "sub"), None, None),
            P(("region", "sub"), None, None),
            P(("region", "sub"), None),
            P(("region", "sub"), None, None, None),
            P(("region", "sub"), None, None),
            P(("region", "sub"), None, None),
            P(("region", "sub"), None),
            P(("region", "sub"), None),
            P(("region", "sub"), None, None),
        ),
        out_specs=(
            P(("region", "sub"), None, None, None),
            P(("region", "sub"), None, None),
            P(("region", "sub"), None, None, None),
        ),
        check_vma=False,
    )
```

```python
import functools
import math

import jax
import jax.numpy as jnp
import numpy as np
from jax import lax
from jax.experimental import pallas as pl
from jax.experimental.pallas import tpu as pltpu
from jax.sharding import PartitionSpec as P

NODES = 2048
NEIGH = 4
LPP = 8
DELAY = 40
SPANS = 2
SCEN = 16
TERM_DEV = 256
BINS = 8
DFT_LEN = 2048

LINES = NEIGH * LPP
COLS = DELAY * SCEN
LANES = 128
PHASOR = 2 * BINS * SCEN
ROWS = 512
VMEM_LIMIT = 32 * 1024 * 1024

F32 = jnp.float32
BF16 = jnp.bfloat16


def fit_table():
    step = np.arange(DELAY)
    harmonic = np.arange(1, BINS + 1)
    angles = (step[:, None] * harmonic[None, :] % DFT_LEN) * (2.0 * math.pi / DFT_LEN)
    twiddle = np.stack([np.cos(angles), -np.sin(angles)], axis=1) / math.sqrt(DFT_LEN)
    table = np.einsum("uch,st->uscht", twiddle, np.eye(SCEN))
    table = table.reshape(COLS, PHASOR).astype(np.float32)
    high = table.astype(jnp.bfloat16)
    low = (table - high.astype(np.float32)).astype(jnp.bfloat16)
    return np.concatenate([high, low], axis=1)


def fit(values, table_ref):
    high, low = split(values)
    both = dot(high, table_ref[...])
    return both[:, :PHASOR] + both[:, PHASOR:] + dot(low, table_ref[:, :PHASOR])


def span_turn():
    angles = 2.0 * math.pi / DFT_LEN * DELAY * np.repeat(np.arange(1, BINS + 1), SCEN)
    return np.stack([np.cos(angles), np.sin(angles)] * 4).astype(np.float32)


def turned(values, turn_ref):
    cosine, sine = turn_ref[0:1, :], turn_ref[1:2, :]
    real, imag = values[:, :LANES], values[:, LANES:]
    return jnp.concatenate([real * cosine + imag * sine, imag * cosine - real * sine], axis=1)


def dot(left, right):
    return jnp.dot(left, right, preferred_element_type=F32)


def split(value):
    high = value.astype(BF16)
    return high, (value - high.astype(F32)).astype(BF16)


def iota(shape, axis):
    return lax.broadcasted_iota(jnp.int32, shape, axis)


def slot_vectors(nodes_ref, admit_ref):
    lane = iota((1, LANES), 1)
    row_id = iota((LINES, 1), 0)
    along = jnp.full((1, LANES), -1, jnp.int32)
    down = jnp.full((LINES, 1), -1, jnp.int32)
    admit = jnp.zeros((LINES, 1), F32)
    for slot in range(LINES):
        node = nodes_ref[0, slot // LPP, slot % LPP]
        along = jnp.where((lane % LINES == slot) & (lane < 3 * LINES), node, along)
        down = jnp.where(row_id == slot, node, down)
        admit = jnp.where(row_id == slot, admit_ref[0, slot // LPP, slot % LPP], admit)
    return along, down, admit


def same_node(along, down):
    return (down == along) & (down >= 0)


def first_along(along, down):
    shape = (LINES, LANES)
    before = same_node(along, down) & (iota(shape, 0) < iota(shape, 1) % LINES)
    return (jnp.sum(jnp.where(before, 1, 0), axis=0, keepdims=True) == 0) & (along >= 0)


def first_down(along, down):
    shape = (LINES, LANES)
    before = same_node(along, down) & (iota(shape, 1) < iota(shape, 0))
    return (jnp.sum(jnp.where(before, 1, 0), axis=1, keepdims=True) == 0) & (down >= 0)


def injected(lines, along, down):
    pick = jnp.where(same_node(along, down), 1.0, 0.0).astype(BF16)[:, : 3 * LINES]
    high = lines.astype(BF16)
    mid, low = split(lines - high.astype(F32))
    total = dot(pick, jnp.concatenate([high, mid, low], axis=0)).astype(BF16)
    return total, jnp.where(first_down(along, down), total, jnp.zeros_like(total))


def three_times(rows):
    width = rows.shape[1]
    return jnp.concatenate([rows, rows, rows, jnp.zeros((LANES - 3 * LINES, width), rows.dtype)], axis=0)


def column_of(row):
    size = row.shape[1]
    eye = iota((size, size), 0) == iota((size, size), 1)
    return jnp.sum(jnp.where(eye, row, 0.0), axis=1, keepdims=True)


def small_left(gathered, self_col, along, first, offset):
    rows = gathered.shape[0]
    lane = iota((1, LANES), 1)
    high, low = split(self_col)
    here = (iota((rows, LANES), 0) + offset == along) & first & (lane >= LINES)
    weight = jnp.where(lane < 2 * LINES, high.astype(F32), low.astype(F32))
    return (gathered + jnp.where(here, weight, 0.0)).astype(BF16)


def send_out(volts, lines, admit, down, place_ref, sub_ref, near_ref, far_ref):
    outgoing = jnp.where(down >= 0, 2.0 * admit * volts - lines, 0.0)
    odd_region = place_ref[0] == 1
    odd_sub = place_ref[1] == 1
    lower_sub, upper_sub = outgoing[:LPP], outgoing[LPP : 2 * LPP]
    lower, upper = outgoing[2 * LPP : 3 * LPP], outgoing[3 * LPP :]
    sub_ref[...] = jnp.where(odd_sub, lower_sub, upper_sub)
    near_ref[...] = jnp.where(odd_region, lower, upper)
    far_ref[...] = jnp.where(odd_region, upper, lower)


def arrived(place_ref, from_far_ref, from_sub_ref, from_near_ref):
    odd_region = place_ref[0] == 1
    odd_sub = place_ref[1] == 1
    from_sub, near, far = from_sub_ref[...], from_near_ref[...], from_far_ref[...]
    none = jnp.zeros_like(from_sub)
    return jnp.concatenate(
        [
            jnp.where(odd_sub, from_sub, none),
            jnp.where(odd_sub, none, from_sub),
            jnp.where(odd_region, near, far),
            jnp.where(odd_region, far, near),
        ],
        axis=0,
    )


def lines_kernel(
    place_ref, nodes_hbm, admit_hbm, self_hbm, history_hbm, coupling_hbm, sources_hbm,
    sub_ref, near_ref, far_ref, src_ref, term_ref, rows_ref, gathered_ref, inj_ref,
    slot_ref, value_ref, self_ref,
    nodes_ref, admit_ref, history_ref, blocks, early_sem, src_sem, late_sem, block_sem,
):
    chunks = 2
    depth = NODES // chunks
    first_cols = pl.ds(0, COLS)

    def early(index, source, target):
        return pltpu.make_async_copy(source, target, early_sem.at[index])

    def src_copy(part):
        rows = pl.ds(part * depth, depth)
        return pltpu.make_async_copy(
            sources_hbm.at[0, rows, first_cols], src_ref.at[rows, first_cols], src_sem.at[part]
        )

    def block_copy(slot):
        node = jnp.maximum(nodes_ref[0, slot // LPP, slot % LPP], 0)
        start = pl.multiple_of((node // 16) * 16, 16)
        return pltpu.make_async_copy(
            coupling_hbm.at[0, pl.ds(start, 16)], blocks.at[pl.ds(slot * 16, 16)], block_sem.at[slot]
        )

    nodes_copy = early(0, nodes_hbm, nodes_ref)
    admit_copy = early(1, admit_hbm, admit_ref)
    self_copy = early(2, self_hbm, self_ref)
    history_copy = early(3, history_hbm, history_ref)
    term_copy = pltpu.make_async_copy(coupling_hbm.at[0, pl.ds(0, TERM_DEV)], term_ref, late_sem)
    nodes_copy.start()
    admit_copy.start()
    self_copy.start()
    history_copy.start()
    for part in range(chunks):
        src_copy(part).start()
    nodes_copy.wait()
    for slot in range(LINES):
        block_copy(slot).start()
    admit_copy.wait()
    self_copy.wait()
    history_copy.wait()

    along, down, admit = slot_vectors(nodes_ref, admit_ref)
    lines = history_ref[0].reshape(LINES, COLS)
    total, injection = injected(lines, along, down)
    inj_ref[...] = injection
    at_node = jnp.maximum(down, 0)
    choose = jnp.where(
        iota((LINES, LINES * 16), 1) == iota((LINES, LINES * 16), 0) * 16 + at_node % 16, 1.0, 0.0
    ).astype(BF16)
    own_row = iota((LINES, NODES), 1) == at_node
    own = jnp.where(own_row, 1.0, 0.0).astype(BF16)
    self_col = jnp.sum(jnp.where(own_row, self_ref[...], 0.0), axis=1, keepdims=True)
    wanted = jnp.where(iota((1, LANES), 1) < LINES, along, -1)
    hot = jnp.where(iota((NODES, LANES), 0) == wanted, 1.0, 0.0).astype(BF16)
    src_ref[:, COLS:] = hot
    slot_ref[:LINES, :] = jnp.broadcast_to(down, (LINES, LANES))
    slot_ref[LINES:, :] = jnp.broadcast_to(along, (8, LANES))
    value_ref[:LINES, :] = jnp.broadcast_to(admit, (LINES, LANES))
    value_ref[LINES:, :] = jnp.broadcast_to(self_col, (LINES, LANES))

    for slot in range(LINES):
        block_copy(slot).wait()
    term_copy.start()
    rows = dot(choose, blocks[...]).astype(BF16)
    rows_ref[...] = rows
    gathered = dot(rows, hot).astype(BF16)
    gathered_ref[...] = gathered
    volts = dot(gathered[:, :LINES], injection)
    left = jnp.concatenate([rows, own], axis=0)
    for part in range(chunks):
        src_copy(part).wait()
    picked = jnp.zeros((2 * LINES, COLS), F32)
    for part in range(chunks):
        span = slice(part * depth, (part + 1) * depth)
        picked = picked + dot(left[:, span], src_ref[span, :COLS])
    volts = volts + picked[:LINES] + self_col * (picked[LINES:] + total.astype(F32))
    send_out(volts, lines, admit, down, place_ref, sub_ref, near_ref, far_ref)
    term_copy.wait()


def terminals_kernel(
    capacity, slots,
    slot_ref, inj_ref, src_ref, term_ref, self_ref, region_ref, prior_ref, old_ref, table_ref, turn_ref,
    sources_ref,
    packed_ref, left_ref,
):
    down = slot_ref[:LINES, :1]
    along = slot_ref[LINES : LINES + 1, :]
    first = first_along(along, down)
    term_self = column_of(self_ref[:, :TERM_DEV])

    products = dot(term_ref[...], src_ref[...])
    small = small_left(products[:, COLS:], term_self, along, first, 0)
    volts = products[:, :COLS] + term_self * src_ref[:TERM_DEV, :COLS].astype(F32)
    volts = volts + dot(small, three_times(inj_ref[...]))

    region_row = region_ref[...]
    region_col = column_of(region_row.astype(F32)).astype(jnp.int32)
    earlier = iota((TERM_DEV, TERM_DEV), 0) < iota((TERM_DEV, TERM_DEV), 1)
    rank = jnp.sum(
        jnp.where((region_col == region_row) & earlier, 1, 0), axis=0, keepdims=True
    )
    dest = region_row * capacity + rank
    pack = jnp.where(iota((slots, TERM_DEV), 0) == dest, 1.0, 0.0).astype(BF16)
    left_ref[...] = dot(pack, small).astype(BF16)

    later = dot(term_ref[...], sources_ref[0, :, COLS:])
    later = later + term_self * sources_ref[0, :TERM_DEV, COLS:].astype(F32)
    running = jnp.concatenate(
        [prior_ref[pl.ds(part, TERM_DEV, stride=2), :] for part in range(2)], axis=1
    )
    first = fit(volts - old_ref[:, :COLS].astype(F32), table_ref)
    second = turned(fit(later - old_ref[:, COLS:].astype(F32), table_ref), turn_ref)
    high, low = split(running + first)
    later_high, later_low = split(running + first + second)
    fitted = jnp.concatenate(
        [
            jnp.concatenate([high, later_high], axis=1),
            jnp.concatenate([low, later_low], axis=1),
        ],
        axis=0,
    )
    filled = dot(jnp.concatenate([pack, pack], axis=1), fitted)
    for part in range(4):
        packed_ref[pl.ds(part, slots, stride=4), :] = filled[:, part * LANES : (part + 1) * LANES]


def second_kernel(
    slots,
    place_ref, slot_ref, from_far_ref, from_sub_ref, from_near_ref, left_ref, table_ref, turn_ref, packed_in_ref,
    packed_hbm,
    packed_ref, sems,
):
    down = slot_ref[:LINES, :1]
    along = slot_ref[LINES : LINES + 1, :]
    lines = arrived(place_ref, from_far_ref, from_sub_ref, from_near_ref)
    _, injection = injected(lines, along, down)
    both = dot(injection, table_ref[...])
    high, low = split(turned(both[:, :PHASOR] + both[:, PHASOR:], turn_ref))
    left = left_ref[...]
    change = dot(
        jnp.concatenate([left, left], axis=1),
        jnp.concatenate([three_times(high), three_times(low)], axis=0),
    )
    chunks = 4
    depth = slots // chunks

    def send(chunk):
        rows = pl.ds(chunk * depth * 4, depth * 4)
        return pltpu.make_async_copy(packed_ref.at[rows], packed_hbm.at[rows], sems.at[chunk])

    for chunk in range(chunks):
        for part in range(4):
            rows = pl.ds(chunk * depth * 4 + part, depth, stride=4)
            values = packed_in_ref[rows, :]
            if part >= 2:
                values = values + change[
                    chunk * depth : (chunk + 1) * depth, (part - 2) * LANES : (part - 1) * LANES
                ]
            packed_ref[rows, :] = values
        send(chunk).start()
    for chunk in range(chunks):
        send(chunk).wait()


def last_lines_kernel(
    place_ref, slot_ref, value_ref, from_far_ref, from_sub_ref, from_near_ref,
    rows_ref, gathered_ref, inj0_ref, nodes_hbm, sources_hbm, coupling_hbm, started_ref,
    sub_ref, near_ref, far_ref, drive_ref, head_ref,
    nodes_ref, sems,
):
    del started_ref
    nodes_copy = pltpu.make_async_copy(nodes_hbm, nodes_ref, sems.at[0])
    head_copy = pltpu.make_async_copy(coupling_hbm.at[0, pl.ds(0, ROWS)], head_ref, sems.at[1])
    copies = [
        pltpu.make_async_copy(
            sources_hbm.at[0, :, pl.ds(span * COLS, COLS)],
            drive_ref.at[:, pl.ds(span * COLS, COLS)],
            sems.at[2 + span],
        )
        for span in range(SPANS)
    ]
    nodes_copy.start()
    copies[1].start()
    copies[0].start()
    head_copy.start()
    down = slot_ref[:LINES, :1]
    along = slot_ref[LINES : LINES + 1, :]
    admit, self_col = value_ref[:LINES, :1], value_ref[LINES:, :1]
    lines = arrived(place_ref, from_far_ref, from_sub_ref, from_near_ref)
    total, injection = injected(lines, along, down)
    own = jnp.where(iota((LINES, NODES), 1) == jnp.maximum(down, 0), 1.0, 0.0).astype(BF16)
    left = jnp.concatenate([rows_ref[...], own], axis=0)
    volts = dot(gathered_ref[:, :LINES], injection)
    nodes_copy.wait()
    copies[1].wait()
    picked = dot(left, drive_ref[:, COLS:])
    volts = volts + picked[:LINES] + self_col * (picked[LINES:] + total.astype(F32))
    send_out(volts, lines, admit, down, place_ref, sub_ref, near_ref, far_ref)

    copies[0].wait()
    both = jnp.concatenate([inj0_ref[...], injection], axis=1).astype(F32)
    for slot in range(LINES):
        node = jnp.maximum(nodes_ref[0, slot // LPP, slot % LPP], 0)
        rows = pl.ds(pl.multiple_of((node // 16) * 16, 16), 16)
        extra = jnp.where(iota((16, 1), 0) == node % 16, both[slot : slot + 1, :], 0.0)
        drive_ref[rows, :] = (drive_ref[rows, :].astype(F32) + extra).astype(BF16)
    head_copy.wait()


def nodes_kernel(
    drive_ref, head_ref, self_ref, coupling_hbm,
    volts_hbm,
    matrix_buf, volts_buf, in_sem, out_sem,
):
    blocks = NODES // ROWS

    def load(block):
        place = block % 2
        return pltpu.make_async_copy(
            coupling_hbm.at[0, pl.ds(block * ROWS, ROWS)], matrix_buf.at[place], in_sem.at[place]
        )

    def store(block):
        place = block % 2
        return pltpu.make_async_copy(
            volts_buf.at[place], volts_hbm.at[0, pl.ds(block * ROWS, ROWS)], out_sem.at[place]
        )

    load(1).start()
    for block in range(blocks):
        if 0 < block:
            load(block).wait()
        if 0 < block < blocks - 1:
            load(block + 1).start()
        if block >= 2:
            store(block - 2).wait()
        span = slice(block * ROWS, (block + 1) * ROWS)
        block_self = jnp.concatenate(
            [
                column_of(self_ref[:, start : start + 256])
                for start in range(block * ROWS, (block + 1) * ROWS, 256)
            ],
            axis=0,
        )
        matrix = head_ref[...] if block == 0 else matrix_buf[block % 2]
        result = dot(matrix, drive_ref[...])
        result = result + block_self * drive_ref[span, :].astype(F32)
        volts_buf[block % 2] = result.astype(BF16)
        store(block).start()
    for block in range(blocks - 2, blocks):
        store(block).wait()


VM = pl.BlockSpec(memory_space=pltpu.VMEM)
SM = pl.BlockSpec(memory_space=pltpu.SMEM)
HB = pl.BlockSpec(memory_space=pltpu.HBM)


def struct(shape, dtype):
    return jax.ShapeDtypeStruct(shape, dtype)


def in_hbm(*arrays):
    return [pltpu.with_memory_space_constraint(array, pltpu.HBM) for array in arrays]


def in_vmem(*arrays):
    return [pltpu.with_memory_space_constraint(array, pltpu.VMEM) for array in arrays]


def params():
    return pltpu.CompilerParams(vmem_limit_bytes=VMEM_LIMIT)


def exchange(sub, near, far):
    subs = lax.axis_size("sub")
    regions = lax.axis_size("region")

    def swap(block, axis, size, first):
        pairs = []
        for low in range(first, size - 1, 2):
            pairs += [(low, low + 1), (low + 1, low)]
        return lax.ppermute(block, axis, pairs)

    return (
        swap(near, "region", regions, 0),
        swap(sub, "sub", subs, 0),
        swap(far, "region", regions, 1),
    )


def body(
    sources,
    coupling,
    self_term,
    history,
    line_nodes,
    line_admit,
    term_region,
    old_samples,
    prior_phasor,
):
    region_count = lax.axis_size("region")
    capacity = max(2, 2 * TERM_DEV // region_count)
    slots = region_count * capacity
    odd_region = lax.axis_index("region") % 2
    odd_sub = lax.axis_index("sub") % 2
    place = jnp.stack([odd_region, odd_sub]).astype(jnp.int32)
    block = struct((LPP, COLS), F32)
    injection = struct((LINES, COLS), BF16)
    DMA = pltpu.SemaphoreType.DMA

    (sub, near, far, src, term, rows, gathered, inj0, slot, value, self_row) = pl.pallas_call(
        lines_kernel,
        out_shape=[
            block, block, block,
            struct((NODES, COLS + LANES), BF16),
            struct((TERM_DEV, NODES), BF16),
            struct((LINES, NODES), BF16),
            struct((LINES, LANES), BF16),
            injection,
            struct((LINES + 8, LANES), jnp.int32),
            struct((2 * LINES, LANES), F32),
            struct((1, NODES), F32),
        ],
        in_specs=[SM] + [HB] * 6,
        out_specs=[VM] * 11,
        scratch_shapes=[
            pltpu.SMEM((1, NEIGH, LPP), jnp.int32),
            pltpu.SMEM((1, NEIGH, LPP), F32),
            pltpu.VMEM((1, NEIGH, LPP, COLS), F32),
            pltpu.VMEM((LINES * 16, NODES), BF16),
            DMA((4,)), DMA((2,)), DMA, DMA((LINES,)),
        ],
        compiler_params=params(),
        name="lines",
    )(place, *in_hbm(line_nodes, line_admit, self_term, history, coupling, sources))
    region = term_region.reshape(1, TERM_DEV)
    prior = prior_phasor.reshape(TERM_DEV * 2, LANES)
    table = jnp.asarray(fit_table())
    turn = jnp.asarray(span_turn())

    from_near, from_sub, from_far = exchange(sub, near, far)

    packed, left = pl.pallas_call(
        functools.partial(terminals_kernel, capacity, slots),
        out_shape=[struct((slots * 4, LANES), F32), struct((slots, LANES), BF16)],
        in_specs=[VM] * 11,
        out_specs=[VM] * 2,
        compiler_params=params(),
        name="terminals",
    )(slot, inj0, src, term, self_row, region, prior, old_samples, table, turn, sources)

    packed = pl.pallas_call(
        functools.partial(second_kernel, slots),
        out_shape=struct((slots * 4, LANES), F32),
        in_specs=[SM] + [VM] * 8,
        out_specs=HB,
        scratch_shapes=[pltpu.VMEM((slots * 4, LANES), F32), DMA((4,))],
        compiler_params=params(),
        name="second",
    )(place, slot, from_far, from_sub, from_near, left, table, turn, packed)

    result = lax.all_to_all(
        packed.reshape(region_count, capacity * 4, LANES),
        "region",
        split_axis=0,
        concat_axis=0,
        tiled=True,
    )
    phasors = result.reshape(slots, SPANS, 2, LANES)

    sub, near, far, drive, head = pl.pallas_call(
        last_lines_kernel,
        out_shape=[
            block, block, block, struct((NODES, SPANS * COLS), BF16), struct((ROWS, NODES), BF16)
        ],
        in_specs=[SM] + [VM] * 8 + [HB] * 3 + [pl.BlockSpec(memory_space=pl.ANY)],
        out_specs=[VM] * 5,
        scratch_shapes=[pltpu.SMEM((1, NEIGH, LPP), jnp.int32), DMA((4,))],
        compiler_params=params(),
        name="last_lines",
    )(
        place, slot, value, from_far, from_sub, from_near, rows, gathered, inj0,
        *in_hbm(line_nodes, sources, coupling), packed,
    )

    from_near, from_sub, from_far = exchange(sub, near, far)
    none = jnp.zeros_like(from_sub)
    next_history = jnp.stack(
        [
            jnp.where(odd_sub == 1, from_sub, none),
            jnp.where(odd_sub == 1, none, from_sub),
            jnp.where(odd_region == 1, from_near, from_far),
            jnp.where(odd_region == 1, from_far, from_near),
        ],
        axis=0,
    )[None]

    node_voltages = pl.pallas_call(
        nodes_kernel,
        out_shape=struct((1, NODES, SPANS * COLS), BF16),
        in_specs=[VM] * 3 + [HB],
        out_specs=HB,
        scratch_shapes=[
            pltpu.VMEM((2, ROWS, NODES), BF16),
            pltpu.VMEM((2, ROWS, SPANS * COLS), BF16),
            DMA((2,)), DMA((2,)),
        ],
        compiler_params=params(),
        cost_estimate=pl.CostEstimate(
            flops=2 * NODES * NODES * SPANS * COLS, bytes_accessed=20_000_000, transcendentals=0
        ),
        name="nodes",
    )(drive, head, self_row, *in_hbm(coupling))
    return (next_history, node_voltages, phasors)


def solution(mesh):
    return jax.shard_map(
        body,
        mesh=mesh,
        in_specs=(
            P(("region", "sub"), None, None),
            P(("region", "sub"), None, None),
            P(("region", "sub"), None),
            P(("region", "sub"), None, None, None),
            P(("region", "sub"), None, None),
            P(("region", "sub"), None, None),
            P(("region", "sub"), None),
            P(("region", "sub"), None),
            P(("region", "sub"), None, None),
        ),
        out_specs=(
            P(("region", "sub"), None, None, None),
            P(("region", "sub"), None, None),
            P(("region", "sub"), None, None, None),
        ),
        check_vma=False,
    )
```

```python
import functools
import math

import jax
import jax.numpy as jnp
import numpy as np
from jax import lax
from jax.experimental import pallas as pl
from jax.experimental.pallas import tpu as pltpu
from jax.sharding import PartitionSpec as P

NODES = 2048
NEIGH = 4
LPP = 8
DELAY = 40
SPANS = 2
SCEN = 16
TERM_DEV = 256
BINS = 8
DFT_LEN = 2048

LINES = NEIGH * LPP
COLS = DELAY * SCEN
LANES = 128
PHASOR = 2 * BINS * SCEN
ROWS = 512
VMEM_LIMIT = 32 * 1024 * 1024

F32 = jnp.float32
BF16 = jnp.bfloat16


def fit_table():
    step = np.arange(DELAY)
    harmonic = np.arange(1, BINS + 1)
    angles = (step[:, None] * harmonic[None, :] % DFT_LEN) * (2.0 * math.pi / DFT_LEN)
    twiddle = np.stack([np.cos(angles), -np.sin(angles)], axis=1) / math.sqrt(DFT_LEN)
    table = np.einsum("uch,st->uscht", twiddle, np.eye(SCEN))
    table = table.reshape(COLS, PHASOR).astype(np.float32)
    high = table.astype(jnp.bfloat16)
    low = (table - high.astype(np.float32)).astype(jnp.bfloat16)
    return np.concatenate([high, low], axis=1)


def fit(values, table_ref):
    high, low = split(values)
    both = dot(high, table_ref[...])
    return both[:, :PHASOR] + both[:, PHASOR:] + dot(low, table_ref[:, :PHASOR])


def span_turn():
    angles = 2.0 * math.pi / DFT_LEN * DELAY * np.repeat(np.arange(1, BINS + 1), SCEN)
    return np.stack([np.cos(angles), np.sin(angles)] * 4).astype(np.float32)


def turned(values, turn_ref):
    cosine, sine = turn_ref[0:1, :], turn_ref[1:2, :]
    real, imag = values[:, :LANES], values[:, LANES:]
    return jnp.concatenate([real * cosine + imag * sine, imag * cosine - real * sine], axis=1)


def dot(left, right):
    return jnp.dot(left, right, preferred_element_type=F32)


def split(value):
    high = value.astype(BF16)
    return high, (value - high.astype(F32)).astype(BF16)


def iota(shape, axis):
    return lax.broadcasted_iota(jnp.int32, shape, axis)


def slot_vectors(nodes_ref, admit_ref):
    lane = iota((1, LANES), 1)
    row_id = iota((LINES, 1), 0)
    along = jnp.full((1, LANES), -1, jnp.int32)
    down = jnp.full((LINES, 1), -1, jnp.int32)
    admit = jnp.zeros((LINES, 1), F32)
    for slot in range(LINES):
        node = nodes_ref[0, slot // LPP, slot % LPP]
        along = jnp.where((lane % LINES == slot) & (lane < 3 * LINES), node, along)
        down = jnp.where(row_id == slot, node, down)
        admit = jnp.where(row_id == slot, admit_ref[0, slot // LPP, slot % LPP], admit)
    return along, down, admit


def same_node(along, down):
    return (down == along) & (down >= 0)


def first_along(along, down):
    shape = (LINES, LANES)
    before = same_node(along, down) & (iota(shape, 0) < iota(shape, 1) % LINES)
    return (jnp.sum(jnp.where(before, 1, 0), axis=0, keepdims=True) == 0) & (along >= 0)


def first_down(along, down):
    shape = (LINES, LANES)
    before = same_node(along, down) & (iota(shape, 1) < iota(shape, 0))
    return (jnp.sum(jnp.where(before, 1, 0), axis=1, keepdims=True) == 0) & (down >= 0)


def injected(lines, along, down):
    pick = jnp.where(same_node(along, down), 1.0, 0.0).astype(BF16)[:, : 3 * LINES]
    high = lines.astype(BF16)
    mid, low = split(lines - high.astype(F32))
    total = dot(pick, jnp.concatenate([high, mid, low], axis=0)).astype(BF16)
    return total, jnp.where(first_down(along, down), total, jnp.zeros_like(total))


def three_times(rows):
    width = rows.shape[1]
    return jnp.concatenate([rows, rows, rows, jnp.zeros((LANES - 3 * LINES, width), rows.dtype)], axis=0)


def column_of(row):
    size = row.shape[1]
    eye = iota((size, size), 0) == iota((size, size), 1)
    return jnp.sum(jnp.where(eye, row, 0.0), axis=1, keepdims=True)


def small_left(gathered, self_col, along, first, offset):
    rows = gathered.shape[0]
    lane = iota((1, LANES), 1)
    high, low = split(self_col)
    here = (iota((rows, LANES), 0) + offset == along) & first & (lane >= LINES)
    weight = jnp.where(lane < 2 * LINES, high.astype(F32), low.astype(F32))
    return (gathered + jnp.where(here, weight, 0.0)).astype(BF16)


def send_out(volts, lines, admit, down, place_ref, sub_ref, near_ref, far_ref):
    outgoing = jnp.where(down >= 0, 2.0 * admit * volts - lines, 0.0)
    odd_region = place_ref[0] == 1
    odd_sub = place_ref[1] == 1
    lower_sub, upper_sub = outgoing[:LPP], outgoing[LPP : 2 * LPP]
    lower, upper = outgoing[2 * LPP : 3 * LPP], outgoing[3 * LPP :]
    sub_ref[...] = jnp.where(odd_sub, lower_sub, upper_sub)
    near_ref[...] = jnp.where(odd_region, lower, upper)
    far_ref[...] = jnp.where(odd_region, upper, lower)


def arrived(place_ref, from_far_ref, from_sub_ref, from_near_ref):
    odd_region = place_ref[0] == 1
    odd_sub = place_ref[1] == 1
    from_sub, near, far = from_sub_ref[...], from_near_ref[...], from_far_ref[...]
    none = jnp.zeros_like(from_sub)
    return jnp.concatenate(
        [
            jnp.where(odd_sub, from_sub, none),
            jnp.where(odd_sub, none, from_sub),
            jnp.where(odd_region, near, far),
            jnp.where(odd_region, far, near),
        ],
        axis=0,
    )


def lines_kernel(
    place_ref, nodes_hbm, admit_hbm, self_hbm, history_hbm, coupling_hbm, sources_hbm,
    sub_ref, near_ref, far_ref, hot_ref, term_ref, rows_ref, gathered_ref, inj_ref,
    slot_ref, value_ref, self_ref,
    src_ref, nodes_ref, admit_ref, history_ref, blocks, early_sem, src_sem, late_sem, block_sem,
):
    chunks = 2
    depth = NODES // chunks
    first_cols = pl.ds(0, COLS)

    def early(index, source, target):
        return pltpu.make_async_copy(source, target, early_sem.at[index])

    def src_copy(part):
        rows = pl.ds(part * depth, depth)
        return pltpu.make_async_copy(
            sources_hbm.at[0, rows, first_cols], src_ref.at[rows], src_sem.at[part]
        )

    def block_copy(slot):
        node = jnp.maximum(nodes_ref[0, slot // LPP, slot % LPP], 0)
        start = pl.multiple_of((node // 16) * 16, 16)
        return pltpu.make_async_copy(
            coupling_hbm.at[0, pl.ds(start, 16)], blocks.at[pl.ds(slot * 16, 16)], block_sem.at[slot]
        )

    nodes_copy = early(0, nodes_hbm, nodes_ref)
    admit_copy = early(1, admit_hbm, admit_ref)
    self_copy = early(2, self_hbm, self_ref)
    history_copy = early(3, history_hbm, history_ref)
    term_copy = pltpu.make_async_copy(coupling_hbm.at[0, pl.ds(0, TERM_DEV)], term_ref, late_sem)
    nodes_copy.start()
    admit_copy.start()
    self_copy.start()
    history_copy.start()
    for part in range(chunks):
        src_copy(part).start()
    nodes_copy.wait()
    for slot in range(LINES):
        block_copy(slot).start()
    admit_copy.wait()
    self_copy.wait()
    history_copy.wait()

    along, down, admit = slot_vectors(nodes_ref, admit_ref)
    lines = history_ref[0].reshape(LINES, COLS)
    total, injection = injected(lines, along, down)
    inj_ref[...] = injection
    at_node = jnp.maximum(down, 0)
    choose = jnp.where(
        iota((LINES, LINES * 16), 1) == iota((LINES, LINES * 16), 0) * 16 + at_node % 16, 1.0, 0.0
    ).astype(BF16)
    own_row = iota((LINES, NODES), 1) == at_node
    own = jnp.where(own_row, 1.0, 0.0).astype(BF16)
    self_col = jnp.sum(jnp.where(own_row, self_ref[...], 0.0), axis=1, keepdims=True)
    wanted = jnp.where(iota((1, LANES), 1) < LINES, along, -1)
    hot = jnp.where(iota((NODES, LANES), 0) == wanted, 1.0, 0.0).astype(BF16)
    hot_ref[...] = hot
    slot_ref[:LINES, :] = jnp.broadcast_to(down, (LINES, LANES))
    slot_ref[LINES:, :] = jnp.broadcast_to(along, (8, LANES))
    value_ref[:LINES, :] = jnp.broadcast_to(admit, (LINES, LANES))
    value_ref[LINES:, :] = jnp.broadcast_to(self_col, (LINES, LANES))

    for slot in range(LINES):
        block_copy(slot).wait()
    term_copy.start()
    rows = dot(choose, blocks[...]).astype(BF16)
    rows_ref[...] = rows
    gathered = dot(rows, hot).astype(BF16)
    gathered_ref[...] = gathered
    volts = dot(gathered[:, :LINES], injection)
    left = jnp.concatenate([rows, own], axis=0)
    for part in range(chunks):
        src_copy(part).wait()
    picked = jnp.zeros((2 * LINES, COLS), F32)
    for part in range(chunks):
        span = slice(part * depth, (part + 1) * depth)
        picked = picked + dot(left[:, span], src_ref[span, :])
    volts = volts + picked[:LINES] + self_col * (picked[LINES:] + total.astype(F32))
    send_out(volts, lines, admit, down, place_ref, sub_ref, near_ref, far_ref)
    term_copy.wait()


def terminals_kernel(
    capacity, slots,
    slot_ref, inj_ref, hot_ref, term_ref, self_ref, region_ref, prior_ref, old_ref, table_ref, turn_ref,
    sources_ref,
    packed_ref, left_ref,
):
    down = slot_ref[:LINES, :1]
    along = slot_ref[LINES : LINES + 1, :]
    first = first_along(along, down)
    term_self = column_of(self_ref[:, :TERM_DEV])

    products = dot(term_ref[...], sources_ref[0])
    products = products + term_self * sources_ref[0, :TERM_DEV, :].astype(F32)
    small = small_left(dot(term_ref[...], hot_ref[...]), term_self, along, first, 0)
    volts = products[:, :COLS] + dot(small, three_times(inj_ref[...]))

    region_row = region_ref[...]
    region_col = column_of(region_row.astype(F32)).astype(jnp.int32)
    earlier = iota((TERM_DEV, TERM_DEV), 0) < iota((TERM_DEV, TERM_DEV), 1)
    rank = jnp.sum(
        jnp.where((region_col == region_row) & earlier, 1, 0), axis=0, keepdims=True
    )
    dest = region_row * capacity + rank
    pack = jnp.where(iota((slots, TERM_DEV), 0) == dest, 1.0, 0.0).astype(BF16)
    left_ref[...] = dot(pack, small).astype(BF16)

    later = products[:, COLS:]
    running = jnp.concatenate(
        [prior_ref[pl.ds(part, TERM_DEV, stride=2), :] for part in range(2)], axis=1
    )
    first = fit(volts - old_ref[:, :COLS].astype(F32), table_ref)
    second = turned(fit(later - old_ref[:, COLS:].astype(F32), table_ref), turn_ref)
    high, low = split(running + first)
    later_high, later_low = split(running + first + second)
    fitted = jnp.concatenate(
        [
            jnp.concatenate([high, later_high], axis=1),
            jnp.concatenate([low, later_low], axis=1),
        ],
        axis=0,
    )
    filled = dot(jnp.concatenate([pack, pack], axis=1), fitted)
    for part in range(4):
        packed_ref[pl.ds(part, slots, stride=4), :] = filled[:, part * LANES : (part + 1) * LANES]


def second_kernel(
    slots,
    place_ref, slot_ref, from_far_ref, from_sub_ref, from_near_ref, left_ref, table_ref, turn_ref, packed_in_ref,
    packed_hbm,
    packed_ref, sems,
):
    down = slot_ref[:LINES, :1]
    along = slot_ref[LINES : LINES + 1, :]
    lines = arrived(place_ref, from_far_ref, from_sub_ref, from_near_ref)
    _, injection = injected(lines, along, down)
    both = dot(injection, table_ref[...])
    high, low = split(turned(both[:, :PHASOR] + both[:, PHASOR:], turn_ref))
    left = left_ref[...]
    change = dot(
        jnp.concatenate([left, left], axis=1),
        jnp.concatenate([three_times(high), three_times(low)], axis=0),
    )
    chunks = 4
    depth = slots // chunks

    def send(chunk):
        rows = pl.ds(chunk * depth * 4, depth * 4)
        return pltpu.make_async_copy(packed_ref.at[rows], packed_hbm.at[rows], sems.at[chunk])

    for chunk in range(chunks):
        for part in range(4):
            rows = pl.ds(chunk * depth * 4 + part, depth, stride=4)
            values = packed_in_ref[rows, :]
            if part >= 2:
                values = values + change[
                    chunk * depth : (chunk + 1) * depth, (part - 2) * LANES : (part - 1) * LANES
                ]
            packed_ref[rows, :] = values
        send(chunk).start()
    for chunk in range(chunks):
        send(chunk).wait()


def last_lines_kernel(
    place_ref, slot_ref, value_ref, from_far_ref, from_sub_ref, from_near_ref,
    rows_ref, gathered_ref, inj0_ref, nodes_hbm, sources_hbm, coupling_hbm, started_ref,
    sub_ref, near_ref, far_ref, drive_ref, head_ref,
    nodes_ref, sems,
):
    del started_ref
    nodes_copy = pltpu.make_async_copy(nodes_hbm, nodes_ref, sems.at[0])
    head_copy = pltpu.make_async_copy(coupling_hbm.at[0, pl.ds(0, ROWS)], head_ref, sems.at[1])
    copies = [
        pltpu.make_async_copy(
            sources_hbm.at[0, :, pl.ds(span * COLS, COLS)],
            drive_ref.at[:, pl.ds(span * COLS, COLS)],
            sems.at[2 + span],
        )
        for span in range(SPANS)
    ]
    nodes_copy.start()
    copies[1].start()
    copies[0].start()
    head_copy.start()
    down = slot_ref[:LINES, :1]
    along = slot_ref[LINES : LINES + 1, :]
    admit, self_col = value_ref[:LINES, :1], value_ref[LINES:, :1]
    lines = arrived(place_ref, from_far_ref, from_sub_ref, from_near_ref)
    total, injection = injected(lines, along, down)
    own = jnp.where(iota((LINES, NODES), 1) == jnp.maximum(down, 0), 1.0, 0.0).astype(BF16)
    left = jnp.concatenate([rows_ref[...], own], axis=0)
    volts = dot(gathered_ref[:, :LINES], injection)
    nodes_copy.wait()
    copies[1].wait()
    picked = dot(left, drive_ref[:, COLS:])
    volts = volts + picked[:LINES] + self_col * (picked[LINES:] + total.astype(F32))
    send_out(volts, lines, admit, down, place_ref, sub_ref, near_ref, far_ref)

    copies[0].wait()
    both = jnp.concatenate([inj0_ref[...], injection], axis=1).astype(F32)
    for slot in range(LINES):
        node = jnp.maximum(nodes_ref[0, slot // LPP, slot % LPP], 0)
        rows = pl.ds(pl.multiple_of((node // 16) * 16, 16), 16)
        extra = jnp.where(iota((16, 1), 0) == node % 16, both[slot : slot + 1, :], 0.0)
        drive_ref[rows, :] = (drive_ref[rows, :].astype(F32) + extra).astype(BF16)
    head_copy.wait()


def nodes_kernel(
    drive_ref, head_ref, self_ref, coupling_hbm,
    volts_hbm,
    matrix_buf, volts_buf, in_sem, out_sem,
):
    blocks = NODES // ROWS

    def load(block):
        place = block % 2
        return pltpu.make_async_copy(
            coupling_hbm.at[0, pl.ds(block * ROWS, ROWS)], matrix_buf.at[place], in_sem.at[place]
        )

    def store(block):
        place = block % 2
        return pltpu.make_async_copy(
            volts_buf.at[place], volts_hbm.at[0, pl.ds(block * ROWS, ROWS)], out_sem.at[place]
        )

    load(1).start()
    for block in range(blocks):
        if 0 < block:
            load(block).wait()
        if 0 < block < blocks - 1:
            load(block + 1).start()
        if block >= 2:
            store(block - 2).wait()
        span = slice(block * ROWS, (block + 1) * ROWS)
        block_self = jnp.concatenate(
            [
                column_of(self_ref[:, start : start + 256])
                for start in range(block * ROWS, (block + 1) * ROWS, 256)
            ],
            axis=0,
        )
        matrix = head_ref[...] if block == 0 else matrix_buf[block % 2]
        result = dot(matrix, drive_ref[...])
        result = result + block_self * drive_ref[span, :].astype(F32)
        volts_buf[block % 2] = result.astype(BF16)
        store(block).start()
    for block in range(blocks - 2, blocks):
        store(block).wait()


VM = pl.BlockSpec(memory_space=pltpu.VMEM)
SM = pl.BlockSpec(memory_space=pltpu.SMEM)
HB = pl.BlockSpec(memory_space=pltpu.HBM)


def struct(shape, dtype):
    return jax.ShapeDtypeStruct(shape, dtype)


def in_hbm(*arrays):
    return [pltpu.with_memory_space_constraint(array, pltpu.HBM) for array in arrays]


def in_vmem(*arrays):
    return [pltpu.with_memory_space_constraint(array, pltpu.VMEM) for array in arrays]


def params():
    return pltpu.CompilerParams(vmem_limit_bytes=VMEM_LIMIT)


def exchange(sub, near, far):
    subs = lax.axis_size("sub")
    regions = lax.axis_size("region")

    def swap(block, axis, size, first):
        pairs = []
        for low in range(first, size - 1, 2):
            pairs += [(low, low + 1), (low + 1, low)]
        return lax.ppermute(block, axis, pairs)

    return (
        swap(near, "region", regions, 0),
        swap(sub, "sub", subs, 0),
        swap(far, "region", regions, 1),
    )


def body(
    sources,
    coupling,
    self_term,
    history,
    line_nodes,
    line_admit,
    term_region,
    old_samples,
    prior_phasor,
):
    region_count = lax.axis_size("region")
    capacity = max(2, 2 * TERM_DEV // region_count)
    slots = region_count * capacity
    odd_region = lax.axis_index("region") % 2
    odd_sub = lax.axis_index("sub") % 2
    place = jnp.stack([odd_region, odd_sub]).astype(jnp.int32)
    block = struct((LPP, COLS), F32)
    injection = struct((LINES, COLS), BF16)
    DMA = pltpu.SemaphoreType.DMA

    (sub, near, far, hot, term, rows, gathered, inj0, slot, value, self_row) = pl.pallas_call(
        lines_kernel,
        out_shape=[
            block, block, block,
            struct((NODES, LANES), BF16),
            struct((TERM_DEV, NODES), BF16),
            struct((LINES, NODES), BF16),
            struct((LINES, LANES), BF16),
            injection,
            struct((LINES + 8, LANES), jnp.int32),
            struct((2 * LINES, LANES), F32),
            struct((1, NODES), F32),
        ],
        in_specs=[SM] + [HB] * 6,
        out_specs=[VM] * 11,
        scratch_shapes=[
            pltpu.VMEM((NODES, COLS), BF16),
            pltpu.SMEM((1, NEIGH, LPP), jnp.int32),
            pltpu.SMEM((1, NEIGH, LPP), F32),
            pltpu.VMEM((1, NEIGH, LPP, COLS), F32),
            pltpu.VMEM((LINES * 16, NODES), BF16),
            DMA((4,)), DMA((2,)), DMA, DMA((LINES,)),
        ],
        compiler_params=params(),
        name="lines",
    )(place, *in_hbm(line_nodes, line_admit, self_term, history, coupling, sources))
    region = term_region.reshape(1, TERM_DEV)
    prior = prior_phasor.reshape(TERM_DEV * 2, LANES)
    table = jnp.asarray(fit_table())
    turn = jnp.asarray(span_turn())

    from_near, from_sub, from_far = exchange(sub, near, far)

    packed, left = pl.pallas_call(
        functools.partial(terminals_kernel, capacity, slots),
        out_shape=[struct((slots * 4, LANES), F32), struct((slots, LANES), BF16)],
        in_specs=[VM] * 11,
        out_specs=[VM] * 2,
        compiler_params=params(),
        name="terminals",
    )(slot, inj0, hot, term, self_row, region, prior, old_samples, table, turn, sources)

    packed = pl.pallas_call(
        functools.partial(second_kernel, slots),
        out_shape=struct((slots * 4, LANES), F32),
        in_specs=[SM] + [VM] * 8,
        out_specs=HB,
        scratch_shapes=[pltpu.VMEM((slots * 4, LANES), F32), DMA((4,))],
        compiler_params=params(),
        name="second",
    )(place, slot, from_far, from_sub, from_near, left, table, turn, packed)

    result = lax.all_to_all(
        packed.reshape(region_count, capacity * 4, LANES),
        "region",
        split_axis=0,
        concat_axis=0,
        tiled=True,
    )
    phasors = result.reshape(slots, SPANS, 2, LANES)

    sub, near, far, drive, head = pl.pallas_call(
        last_lines_kernel,
        out_shape=[
            block, block, block, struct((NODES, SPANS * COLS), BF16), struct((ROWS, NODES), BF16)
        ],
        in_specs=[SM] + [VM] * 8 + [HB] * 3 + [pl.BlockSpec(memory_space=pl.ANY)],
        out_specs=[VM] * 5,
        scratch_shapes=[pltpu.SMEM((1, NEIGH, LPP), jnp.int32), DMA((4,))],
        compiler_params=params(),
        name="last_lines",
    )(
        place, slot, value, from_far, from_sub, from_near, rows, gathered, inj0,
        *in_hbm(line_nodes, sources, coupling), packed,
    )

    from_near, from_sub, from_far = exchange(sub, near, far)
    none = jnp.zeros_like(from_sub)
    next_history = jnp.stack(
        [
            jnp.where(odd_sub == 1, from_sub, none),
            jnp.where(odd_sub == 1, none, from_sub),
            jnp.where(odd_region == 1, from_near, from_far),
            jnp.where(odd_region == 1, from_far, from_near),
        ],
        axis=0,
    )[None]

    node_voltages = pl.pallas_call(
        nodes_kernel,
        out_shape=struct((1, NODES, SPANS * COLS), BF16),
        in_specs=[VM] * 3 + [HB],
        out_specs=HB,
        scratch_shapes=[
            pltpu.VMEM((2, ROWS, NODES), BF16),
            pltpu.VMEM((2, ROWS, SPANS * COLS), BF16),
            DMA((2,)), DMA((2,)),
        ],
        compiler_params=params(),
        cost_estimate=pl.CostEstimate(
            flops=2 * NODES * NODES * SPANS * COLS, bytes_accessed=20_000_000, transcendentals=0
        ),
        name="nodes",
    )(drive, head, self_row, *in_hbm(coupling))
    return (next_history, node_voltages, phasors)


def solution(mesh):
    return jax.shard_map(
        body,
        mesh=mesh,
        in_specs=(
            P(("region", "sub"), None, None),
            P(("region", "sub"), None, None),
            P(("region", "sub"), None),
            P(("region", "sub"), None, None, None),
            P(("region", "sub"), None, None),
            P(("region", "sub"), None, None),
            P(("region", "sub"), None),
            P(("region", "sub"), None),
            P(("region", "sub"), None, None),
        ),
        out_specs=(
            P(("region", "sub"), None, None, None),
            P(("region", "sub"), None, None),
            P(("region", "sub"), None, None, None),
        ),
        check_vma=False,
    )
```

```python
import functools
import math

import jax
import jax.numpy as jnp
import numpy as np
from jax import lax
from jax.experimental import pallas as pl
from jax.experimental.pallas import tpu as pltpu
from jax.sharding import PartitionSpec as P

NODES = 2048
NEIGH = 4
LPP = 8
DELAY = 40
SPANS = 2
SCEN = 16
TERM_DEV = 256
BINS = 8
DFT_LEN = 2048

LINES = NEIGH * LPP
COLS = DELAY * SCEN
LANES = 128
PHASOR = 2 * BINS * SCEN
ROWS = 512
VMEM_LIMIT = 32 * 1024 * 1024

F32 = jnp.float32
BF16 = jnp.bfloat16


def fit_table():
    step = np.arange(DELAY)
    harmonic = np.arange(1, BINS + 1)
    angles = (step[:, None] * harmonic[None, :] % DFT_LEN) * (2.0 * math.pi / DFT_LEN)
    twiddle = np.stack([np.cos(angles), -np.sin(angles)], axis=1) / math.sqrt(DFT_LEN)
    table = np.einsum("uch,st->uscht", twiddle, np.eye(SCEN))
    table = table.reshape(COLS, PHASOR).astype(np.float32)
    high = table.astype(jnp.bfloat16)
    low = (table - high.astype(np.float32)).astype(jnp.bfloat16)
    return np.concatenate([high, low], axis=1)


def fit(values, table_ref):
    high, low = split(values)
    both = dot(high, table_ref[...])
    return both[:, :PHASOR] + both[:, PHASOR:] + dot(low, table_ref[:, :PHASOR])


def span_turn():
    angles = 2.0 * math.pi / DFT_LEN * DELAY * np.repeat(np.arange(1, BINS + 1), SCEN)
    return np.stack([np.cos(angles), np.sin(angles)] * 4).astype(np.float32)


def turned(values, turn_ref):
    cosine, sine = turn_ref[0:1, :], turn_ref[1:2, :]
    real, imag = values[:, :LANES], values[:, LANES:]
    return jnp.concatenate([real * cosine + imag * sine, imag * cosine - real * sine], axis=1)


def dot(left, right):
    return jnp.dot(left, right, preferred_element_type=F32)


def split(value):
    high = value.astype(BF16)
    return high, (value - high.astype(F32)).astype(BF16)


def iota(shape, axis):
    return lax.broadcasted_iota(jnp.int32, shape, axis)


def slot_vectors(nodes_ref, admit_ref):
    lane = iota((1, LANES), 1)
    row_id = iota((LINES, 1), 0)
    along = jnp.full((1, LANES), -1, jnp.int32)
    down = jnp.full((LINES, 1), -1, jnp.int32)
    admit = jnp.zeros((LINES, 1), F32)
    for slot in range(LINES):
        node = nodes_ref[0, slot // LPP, slot % LPP]
        along = jnp.where((lane % LINES == slot) & (lane < 3 * LINES), node, along)
        down = jnp.where(row_id == slot, node, down)
        admit = jnp.where(row_id == slot, admit_ref[0, slot // LPP, slot % LPP], admit)
    return along, down, admit


def same_node(along, down):
    return (down == along) & (down >= 0)


def first_along(along, down):
    shape = (LINES, LANES)
    before = same_node(along, down) & (iota(shape, 0) < iota(shape, 1) % LINES)
    return (jnp.sum(jnp.where(before, 1, 0), axis=0, keepdims=True) == 0) & (along >= 0)


def first_down(along, down):
    shape = (LINES, LANES)
    before = same_node(along, down) & (iota(shape, 1) < iota(shape, 0))
    return (jnp.sum(jnp.where(before, 1, 0), axis=1, keepdims=True) == 0) & (down >= 0)


def injected(lines, along, down):
    pick = jnp.where(same_node(along, down), 1.0, 0.0).astype(BF16)[:, : 3 * LINES]
    high = lines.astype(BF16)
    mid, low = split(lines - high.astype(F32))
    total = dot(pick, jnp.concatenate([high, mid, low], axis=0)).astype(BF16)
    return total, jnp.where(first_down(along, down), total, jnp.zeros_like(total))


def three_times(rows):
    width = rows.shape[1]
    return jnp.concatenate([rows, rows, rows, jnp.zeros((LANES - 3 * LINES, width), rows.dtype)], axis=0)


def column_of(row):
    size = row.shape[1]
    eye = iota((size, size), 0) == iota((size, size), 1)
    return jnp.sum(jnp.where(eye, row, 0.0), axis=1, keepdims=True)


def small_left(gathered, self_col, along, first, offset):
    rows = gathered.shape[0]
    lane = iota((1, LANES), 1)
    high, low = split(self_col)
    here = (iota((rows, LANES), 0) + offset == along) & first & (lane >= LINES)
    weight = jnp.where(lane < 2 * LINES, high.astype(F32), low.astype(F32))
    return (gathered + jnp.where(here, weight, 0.0)).astype(BF16)


def send_out(volts, lines, admit, down, place_ref, sub_ref, near_ref, far_ref):
    outgoing = jnp.where(down >= 0, 2.0 * admit * volts - lines, 0.0)
    odd_region = place_ref[0] == 1
    odd_sub = place_ref[1] == 1
    lower_sub, upper_sub = outgoing[:LPP], outgoing[LPP : 2 * LPP]
    lower, upper = outgoing[2 * LPP : 3 * LPP], outgoing[3 * LPP :]
    sub_ref[...] = jnp.where(odd_sub, lower_sub, upper_sub)
    near_ref[...] = jnp.where(odd_region, lower, upper)
    far_ref[...] = jnp.where(odd_region, upper, lower)


def arrived(place_ref, from_far_ref, from_sub_ref, from_near_ref):
    odd_region = place_ref[0] == 1
    odd_sub = place_ref[1] == 1
    from_sub, near, far = from_sub_ref[...], from_near_ref[...], from_far_ref[...]
    none = jnp.zeros_like(from_sub)
    return jnp.concatenate(
        [
            jnp.where(odd_sub, from_sub, none),
            jnp.where(odd_sub, none, from_sub),
            jnp.where(odd_region, near, far),
            jnp.where(odd_region, far, near),
        ],
        axis=0,
    )


def lines_kernel(
    place_ref, nodes_hbm, admit_hbm, self_hbm, history_hbm, coupling_hbm, sources_hbm,
    sub_ref, near_ref, far_ref, hot_ref, term_ref, rows_ref, gathered_ref, inj_ref,
    slot_ref, value_ref, self_ref,
    src_ref, nodes_ref, admit_ref, history_ref, blocks, early_sem, src_sem, late_sem, block_sem,
):
    chunks = 2
    depth = NODES // chunks
    first_cols = pl.ds(0, COLS)

    def early(index, source, target):
        return pltpu.make_async_copy(source, target, early_sem.at[index])

    def src_copy(part):
        rows = pl.ds(part * depth, depth)
        return pltpu.make_async_copy(
            sources_hbm.at[0, rows, first_cols], src_ref.at[rows], src_sem.at[part]
        )

    def block_copy(slot):
        node = jnp.maximum(nodes_ref[0, slot // LPP, slot % LPP], 0)
        start = pl.multiple_of((node // 16) * 16, 16)
        return pltpu.make_async_copy(
            coupling_hbm.at[0, pl.ds(start, 16)], blocks.at[pl.ds(slot * 16, 16)], block_sem.at[slot]
        )

    nodes_copy = early(0, nodes_hbm, nodes_ref)
    admit_copy = early(1, admit_hbm, admit_ref)
    self_copy = early(2, self_hbm, self_ref)
    history_copy = early(3, history_hbm, history_ref)
    term_copy = pltpu.make_async_copy(coupling_hbm.at[0, pl.ds(0, TERM_DEV)], term_ref, late_sem)
    nodes_copy.start()
    admit_copy.start()
    self_copy.start()
    history_copy.start()
    for part in range(chunks):
        src_copy(part).start()
    nodes_copy.wait()
    for slot in range(LINES):
        block_copy(slot).start()
    admit_copy.wait()
    self_copy.wait()
    history_copy.wait()

    along, down, admit = slot_vectors(nodes_ref, admit_ref)
    lines = history_ref[0].reshape(LINES, COLS)
    total, injection = injected(lines, along, down)
    inj_ref[...] = injection
    at_node = jnp.maximum(down, 0)
    choose = jnp.where(
        iota((LINES, LINES * 16), 1) == iota((LINES, LINES * 16), 0) * 16 + at_node % 16, 1.0, 0.0
    ).astype(BF16)
    own_row = iota((LINES, NODES), 1) == at_node
    own = jnp.where(own_row, 1.0, 0.0).astype(BF16)
    self_col = jnp.sum(jnp.where(own_row, self_ref[...], 0.0), axis=1, keepdims=True)
    wanted = jnp.where(iota((1, LANES), 1) < LINES, along, -1)
    hot = jnp.where(iota((NODES, LANES), 0) == wanted, 1.0, 0.0).astype(BF16)
    hot_ref[...] = hot
    slot_ref[:LINES, :] = jnp.broadcast_to(down, (LINES, LANES))
    slot_ref[LINES:, :] = jnp.broadcast_to(along, (8, LANES))
    value_ref[:LINES, :] = jnp.broadcast_to(admit, (LINES, LANES))
    value_ref[LINES:, :] = jnp.broadcast_to(self_col, (LINES, LANES))

    for slot in range(LINES):
        block_copy(slot).wait()
    term_copy.start()
    rows = dot(choose, blocks[...]).astype(BF16)
    rows_ref[...] = rows
    gathered = dot(rows, hot).astype(BF16)
    gathered_ref[...] = gathered
    volts = dot(gathered[:, :LINES], injection)
    left = jnp.concatenate([rows, own], axis=0)
    for part in range(chunks):
        src_copy(part).wait()
    picked = jnp.zeros((2 * LINES, COLS), F32)
    for part in range(chunks):
        span = slice(part * depth, (part + 1) * depth)
        picked = picked + dot(left[:, span], src_ref[span, :])
    volts = volts + picked[:LINES] + self_col * (picked[LINES:] + total.astype(F32))
    send_out(volts, lines, admit, down, place_ref, sub_ref, near_ref, far_ref)
    term_copy.wait()


def terminals_kernel(
    capacity, slots,
    slot_ref, inj_ref, hot_ref, term_ref, self_ref, region_ref, prior_ref, old_ref, table_ref, turn_ref,
    sources_ref,
    packed_ref, left_ref,
):
    down = slot_ref[:LINES, :1]
    along = slot_ref[LINES : LINES + 1, :]
    first = first_along(along, down)
    term_self = column_of(self_ref[:, :TERM_DEV])

    products = dot(term_ref[...], sources_ref[0])
    products = products + term_self * sources_ref[0, :TERM_DEV, :].astype(F32)
    small = small_left(dot(term_ref[...], hot_ref[...]), term_self, along, first, 0)
    volts = products[:, :COLS] + dot(small, three_times(inj_ref[...]))

    region_row = region_ref[...]
    region_col = column_of(region_row.astype(F32)).astype(jnp.int32)
    earlier = iota((TERM_DEV, TERM_DEV), 0) < iota((TERM_DEV, TERM_DEV), 1)
    rank = jnp.sum(
        jnp.where((region_col == region_row) & earlier, 1, 0), axis=0, keepdims=True
    )
    dest = region_row * capacity + rank
    pack = jnp.where(iota((slots, TERM_DEV), 0) == dest, 1.0, 0.0).astype(BF16)
    left_ref[...] = dot(pack, small).astype(BF16)

    later = products[:, COLS:]
    running = jnp.concatenate(
        [prior_ref[pl.ds(part, TERM_DEV, stride=2), :] for part in range(2)], axis=1
    )
    first = fit(volts - old_ref[:, :COLS].astype(F32), table_ref)
    second = turned(fit(later - old_ref[:, COLS:].astype(F32), table_ref), turn_ref)
    high, low = split(running + first)
    later_high, later_low = split(running + first + second)
    fitted = jnp.concatenate(
        [
            jnp.concatenate([high, later_high], axis=1),
            jnp.concatenate([low, later_low], axis=1),
        ],
        axis=0,
    )
    filled = dot(jnp.concatenate([pack, pack], axis=1), fitted)
    for part in range(4):
        packed_ref[pl.ds(part, slots, stride=4), :] = filled[:, part * LANES : (part + 1) * LANES]


def second_kernel(
    slots,
    place_ref, slot_ref, from_far_ref, from_sub_ref, from_near_ref, left_ref, table_ref, turn_ref, packed_in_ref,
    packed_hbm,
    packed_ref, sems,
):
    down = slot_ref[:LINES, :1]
    along = slot_ref[LINES : LINES + 1, :]
    lines = arrived(place_ref, from_far_ref, from_sub_ref, from_near_ref)
    _, injection = injected(lines, along, down)
    both = dot(injection, table_ref[...])
    high, low = split(turned(both[:, :PHASOR] + both[:, PHASOR:], turn_ref))
    right = jnp.concatenate([three_times(high), three_times(low)], axis=0)
    chunks = 4
    depth = slots // chunks

    def send(chunk):
        rows = pl.ds(chunk * depth * 4, depth * 4)
        return pltpu.make_async_copy(packed_ref.at[rows], packed_hbm.at[rows], sems.at[chunk])

    for chunk in range(chunks):
        left = left_ref[chunk * depth : (chunk + 1) * depth, :]
        change = dot(jnp.concatenate([left, left], axis=1), right)
        for part in range(4):
            rows = pl.ds(chunk * depth * 4 + part, depth, stride=4)
            values = packed_in_ref[rows, :]
            if part >= 2:
                values = values + change[:, (part - 2) * LANES : (part - 1) * LANES]
            packed_ref[rows, :] = values
        send(chunk).start()
    for chunk in range(chunks):
        send(chunk).wait()


def last_lines_kernel(
    place_ref, slot_ref, value_ref, from_far_ref, from_sub_ref, from_near_ref,
    rows_ref, gathered_ref, inj0_ref, nodes_hbm, sources_hbm, coupling_hbm, started_ref,
    sub_ref, near_ref, far_ref, drive_ref, head_ref,
    nodes_ref, sems,
):
    del started_ref
    nodes_copy = pltpu.make_async_copy(nodes_hbm, nodes_ref, sems.at[0])
    head_copy = pltpu.make_async_copy(coupling_hbm.at[0, pl.ds(0, ROWS)], head_ref, sems.at[1])
    copies = [
        pltpu.make_async_copy(
            sources_hbm.at[0, :, pl.ds(span * COLS, COLS)],
            drive_ref.at[:, pl.ds(span * COLS, COLS)],
            sems.at[2 + span],
        )
        for span in range(SPANS)
    ]
    nodes_copy.start()
    copies[1].start()
    copies[0].start()
    head_copy.start()
    down = slot_ref[:LINES, :1]
    along = slot_ref[LINES : LINES + 1, :]
    admit, self_col = value_ref[:LINES, :1], value_ref[LINES:, :1]
    lines = arrived(place_ref, from_far_ref, from_sub_ref, from_near_ref)
    total, injection = injected(lines, along, down)
    own = jnp.where(iota((LINES, NODES), 1) == jnp.maximum(down, 0), 1.0, 0.0).astype(BF16)
    left = jnp.concatenate([rows_ref[...], own], axis=0)
    volts = dot(gathered_ref[:, :LINES], injection)
    nodes_copy.wait()
    copies[1].wait()
    picked = dot(left, drive_ref[:, COLS:])
    volts = volts + picked[:LINES] + self_col * (picked[LINES:] + total.astype(F32))
    send_out(volts, lines, admit, down, place_ref, sub_ref, near_ref, far_ref)

    copies[0].wait()
    both = jnp.concatenate([inj0_ref[...], injection], axis=1).astype(F32)
    for slot in range(LINES):
        node = jnp.maximum(nodes_ref[0, slot // LPP, slot % LPP], 0)
        rows = pl.ds(pl.multiple_of((node // 16) * 16, 16), 16)
        extra = jnp.where(iota((16, 1), 0) == node % 16, both[slot : slot + 1, :], 0.0)
        drive_ref[rows, :] = (drive_ref[rows, :].astype(F32) + extra).astype(BF16)
    head_copy.wait()


def nodes_kernel(
    drive_ref, head_ref, self_ref, coupling_hbm,
    volts_hbm,
    matrix_buf, volts_buf, in_sem, out_sem,
):
    blocks = NODES // ROWS

    def load(block):
        place = block % 2
        return pltpu.make_async_copy(
            coupling_hbm.at[0, pl.ds(block * ROWS, ROWS)], matrix_buf.at[place], in_sem.at[place]
        )

    def store(block):
        place = block % 2
        return pltpu.make_async_copy(
            volts_buf.at[place], volts_hbm.at[0, pl.ds(block * ROWS, ROWS)], out_sem.at[place]
        )

    load(1).start()
    for block in range(blocks):
        if 0 < block:
            load(block).wait()
        if 0 < block < blocks - 1:
            load(block + 1).start()
        if block >= 2:
            store(block - 2).wait()
        span = slice(block * ROWS, (block + 1) * ROWS)
        block_self = jnp.concatenate(
            [
                column_of(self_ref[:, start : start + 256])
                for start in range(block * ROWS, (block + 1) * ROWS, 256)
            ],
            axis=0,
        )
        matrix = head_ref[...] if block == 0 else matrix_buf[block % 2]
        result = dot(matrix, drive_ref[...])
        result = result + block_self * drive_ref[span, :].astype(F32)
        volts_buf[block % 2] = result.astype(BF16)
        store(block).start()
    for block in range(blocks - 2, blocks):
        store(block).wait()


VM = pl.BlockSpec(memory_space=pltpu.VMEM)
SM = pl.BlockSpec(memory_space=pltpu.SMEM)
HB = pl.BlockSpec(memory_space=pltpu.HBM)


def struct(shape, dtype):
    return jax.ShapeDtypeStruct(shape, dtype)


def in_hbm(*arrays):
    return [pltpu.with_memory_space_constraint(array, pltpu.HBM) for array in arrays]


def in_vmem(*arrays):
    return [pltpu.with_memory_space_constraint(array, pltpu.VMEM) for array in arrays]


def params():
    return pltpu.CompilerParams(vmem_limit_bytes=VMEM_LIMIT)


def exchange(sub, near, far):
    subs = lax.axis_size("sub")
    regions = lax.axis_size("region")

    def swap(block, axis, size, first):
        pairs = []
        for low in range(first, size - 1, 2):
            pairs += [(low, low + 1), (low + 1, low)]
        return lax.ppermute(block, axis, pairs)

    return (
        swap(near, "region", regions, 0),
        swap(sub, "sub", subs, 0),
        swap(far, "region", regions, 1),
    )


def body(
    sources,
    coupling,
    self_term,
    history,
    line_nodes,
    line_admit,
    term_region,
    old_samples,
    prior_phasor,
):
    region_count = lax.axis_size("region")
    capacity = max(2, 2 * TERM_DEV // region_count)
    slots = region_count * capacity
    odd_region = lax.axis_index("region") % 2
    odd_sub = lax.axis_index("sub") % 2
    place = jnp.stack([odd_region, odd_sub]).astype(jnp.int32)
    block = struct((LPP, COLS), F32)
    injection = struct((LINES, COLS), BF16)
    DMA = pltpu.SemaphoreType.DMA

    (sub, near, far, hot, term, rows, gathered, inj0, slot, value, self_row) = pl.pallas_call(
        lines_kernel,
        out_shape=[
            block, block, block,
            struct((NODES, LANES), BF16),
            struct((TERM_DEV, NODES), BF16),
            struct((LINES, NODES), BF16),
            struct((LINES, LANES), BF16),
            injection,
            struct((LINES + 8, LANES), jnp.int32),
            struct((2 * LINES, LANES), F32),
            struct((1, NODES), F32),
        ],
        in_specs=[SM] + [HB] * 6,
        out_specs=[VM] * 11,
        scratch_shapes=[
            pltpu.VMEM((NODES, COLS), BF16),
            pltpu.SMEM((1, NEIGH, LPP), jnp.int32),
            pltpu.SMEM((1, NEIGH, LPP), F32),
            pltpu.VMEM((1, NEIGH, LPP, COLS), F32),
            pltpu.VMEM((LINES * 16, NODES), BF16),
            DMA((4,)), DMA((2,)), DMA, DMA((LINES,)),
        ],
        compiler_params=params(),
        name="lines",
    )(place, *in_hbm(line_nodes, line_admit, self_term, history, coupling, sources))
    region = term_region.reshape(1, TERM_DEV)
    prior = prior_phasor.reshape(TERM_DEV * 2, LANES)
    table = jnp.asarray(fit_table())
    turn = jnp.asarray(span_turn())

    from_near, from_sub, from_far = exchange(sub, near, far)

    packed, left = pl.pallas_call(
        functools.partial(terminals_kernel, capacity, slots),
        out_shape=[struct((slots * 4, LANES), F32), struct((slots, LANES), BF16)],
        in_specs=[VM] * 11,
        out_specs=[VM] * 2,
        compiler_params=params(),
        name="terminals",
    )(slot, inj0, hot, term, self_row, region, prior, old_samples, table, turn, sources)

    packed = pl.pallas_call(
        functools.partial(second_kernel, slots),
        out_shape=struct((slots * 4, LANES), F32),
        in_specs=[SM] + [VM] * 8,
        out_specs=HB,
        scratch_shapes=[pltpu.VMEM((slots * 4, LANES), F32), DMA((4,))],
        compiler_params=params(),
        name="second",
    )(place, slot, from_far, from_sub, from_near, left, table, turn, packed)

    result = lax.all_to_all(
        packed.reshape(region_count, capacity * 4, LANES),
        "region",
        split_axis=0,
        concat_axis=0,
        tiled=True,
    )
    phasors = result.reshape(slots, SPANS, 2, LANES)

    sub, near, far, drive, head = pl.pallas_call(
        last_lines_kernel,
        out_shape=[
            block, block, block, struct((NODES, SPANS * COLS), BF16), struct((ROWS, NODES), BF16)
        ],
        in_specs=[SM] + [VM] * 8 + [HB] * 3 + [pl.BlockSpec(memory_space=pl.ANY)],
        out_specs=[VM] * 5,
        scratch_shapes=[pltpu.SMEM((1, NEIGH, LPP), jnp.int32), DMA((4,))],
        compiler_params=params(),
        name="last_lines",
    )(
        place, slot, value, from_far, from_sub, from_near, rows, gathered, inj0,
        *in_hbm(line_nodes, sources, coupling), packed,
    )

    from_near, from_sub, from_far = exchange(sub, near, far)
    none = jnp.zeros_like(from_sub)
    next_history = jnp.stack(
        [
            jnp.where(odd_sub == 1, from_sub, none),
            jnp.where(odd_sub == 1, none, from_sub),
            jnp.where(odd_region == 1, from_near, from_far),
            jnp.where(odd_region == 1, from_far, from_near),
        ],
        axis=0,
    )[None]

    node_voltages = pl.pallas_call(
        nodes_kernel,
        out_shape=struct((1, NODES, SPANS * COLS), BF16),
        in_specs=[VM] * 3 + [HB],
        out_specs=HB,
        scratch_shapes=[
            pltpu.VMEM((2, ROWS, NODES), BF16),
            pltpu.VMEM((2, ROWS, SPANS * COLS), BF16),
            DMA((2,)), DMA((2,)),
        ],
        compiler_params=params(),
        cost_estimate=pl.CostEstimate(
            flops=2 * NODES * NODES * SPANS * COLS, bytes_accessed=20_000_000, transcendentals=0
        ),
        name="nodes",
    )(drive, head, self_row, *in_hbm(coupling))
    return (next_history, node_voltages, phasors)


def solution(mesh):
    return jax.shard_map(
        body,
        mesh=mesh,
        in_specs=(
            P(("region", "sub"), None, None),
            P(("region", "sub"), None, None),
            P(("region", "sub"), None),
            P(("region", "sub"), None, None, None),
            P(("region", "sub"), None, None),
            P(("region", "sub"), None, None),
            P(("region", "sub"), None),
            P(("region", "sub"), None),
            P(("region", "sub"), None, None),
        ),
        out_specs=(
            P(("region", "sub"), None, None, None),
            P(("region", "sub"), None, None),
            P(("region", "sub"), None, None, None),
        ),
        check_vma=False,
    )
```
